32 devices in a mesh: groups: 1, gx: 32 (over z, y, x, core).
Axes of the slice: x: 2, y: 2, z: 4, core: 2. Of those that a mesh axis runs over, the one named last changes fastest.
Arguments:
- hidden_field: bfloat16 [128, 32, 64, 512], P(('groups', 'gx')), may hold values from -6 to 6
- cotangent: bfloat16 [128, 32, 64, 512], P(('groups', 'gx')), may hold values from -6 to 6
- spectral_weight: bfloat16 [1024, 2, 32, 512], P('gx'), may hold values from -6 to 6
- local_weight: bfloat16 [32, 32], replicated, may hold values from -1 to 1
- local_bias: float32 [32], replicated, may hold values from -3 to 3
Outputs:
- output: bfloat16 [128, 32, 64, 512], P(('groups', 'gx'))
- grad_field: bfloat16 [128, 32, 64, 512], P(('groups', 'gx'))
- grad_spectral: float32 [1024, 2, 32, 512], P('gx', 'groups')
- grad_local: float32 [32, 32], P('groups')
- grad_bias: float32 [32], P('groups')
The draws below stay inside these ranges and needn't reach their ends.
All inputs are finite; a program needn't handle non-finite values.
Results may differ from the reference program's by a relative error of at most 0.0058.
Values sent between devices are 32-bit elements; how exact they have to be, the bound alone decides.
No kernel may reach another device: no remote copies, remote signals or barrier semaphores. Data moves between devices by JAX's collectives and lax.ppermute only.
A program may use at most 192 MiB of HBM per device.

```python
import math
import jax
import jax.numpy as jnp
from jax import lax

NX = 128
NY = 64
NZ = 64
NT = 8
C = 32
KX = 16
KY = 16
KZ = 16
KT = 4


def level_of(own_key, extent, pieces, smallest, top_value):
    gain, own = 1.0, jax.random.fold_in(own_key, 6)
    for position, shards_of in pieces:
        steps = jnp.exp(jax.random.uniform(jax.random.fold_in(own, position), (shards_of,), jnp.float32, smallest / len(pieces), top_value / len(pieces)))
        gain = gain * jnp.repeat(steps, extent[position] // shards_of).reshape([-1 if axis == position else 1 for axis in range(len(extent))])
    return gain


def centred(key, shape, spread, reach, pieces=(), kind=jnp.bfloat16):
    values = jax.random.normal(key, shape, jnp.float32) * spread
    if len(pieces) > 0:
        values = level_of(key, shape, pieces, -0.22, 0.18) * values
    return jnp.clip(values, min=-reach, max=reach).astype(kind)


def setup_inputs(seed: int = 0, part: int = 0) -> dict:
    keys = jax.random.split(jax.random.key(seed), 6)
    own_keys = jax.random.split(jax.random.fold_in(keys[5], part), 6)
    return {
        "hidden_field": centred(own_keys[0], (NX, C, NY, NZ * NT), 1.0, 6.0, ((0, 32),)),
        "cotangent": centred(own_keys[1], (NX, C, NY, NZ * NT), 1.0, 6.0, ((0, 32),)),
        "spectral_weight": centred(keys[2], (KY * KZ * KT, 2, C, KX * C), 1.0, 6.0, ((0, 32),)),
        "local_weight": centred(keys[3], (C, C), C ** -0.5, 1.0),
        "local_bias": centred(keys[4], (C,), 0.5, 3.0, (), jnp.float32),
    }


HIGHEST = lax.Precision.HIGHEST

def kept_frequency(kept):
    serial = jnp.arange(kept, dtype=jnp.int32)
    return jnp.where(serial < kept // 2, serial, serial - kept)

def axis_tables(positions, length, kept):
    wound = positions[:, None] * kept_frequency(kept)[None, :] % length
    angles = 2.0 * math.pi / length * wound.astype(jnp.float32)
    return (jnp.cos(angles), jnp.sin(angles))

def joint_table():
    cells = jnp.arange(NZ * NT, dtype=jnp.int32)
    depth = cells // NT
    moment = cells % NT
    kept_z = jnp.repeat(kept_frequency(KZ), KT)
    kept_t = jnp.tile(jnp.arange(KT, dtype=jnp.int32), KZ)
    wound = depth[:, None] * kept_z[None, :] % NZ * NT + moment[:, None] * kept_t[None, :] % NT * NZ
    angles = 2.0 * math.pi / (NZ * NT) * (wound % (NZ * NT)).astype(jnp.float32)
    return jnp.concatenate([jnp.cos(angles), -jnp.sin(angles)], axis=1).astype(jnp.bfloat16)

def forward_planes(values, joint, y_cosine, y_sine):
    mixed_zt = jnp.einsum('xcyp,pq->xcyq', values.astype(jnp.float32), joint.astype(jnp.float32), precision=HIGHEST)
    half = mixed_zt.shape[-1] // 2
    real_part = mixed_zt[..., :half]
    imag_part = mixed_zt[..., half:]
    out_real = jnp.einsum('xcym,yk->xckm', real_part, y_cosine, precision=HIGHEST) + jnp.einsum('xcym,yk->xckm', imag_part, y_sine, precision=HIGHEST)
    out_imag = jnp.einsum('xcym,yk->xckm', imag_part, y_cosine, precision=HIGHEST) - jnp.einsum('xcym,yk->xckm', real_part, y_sine, precision=HIGHEST)
    stacked = jnp.stack([out_real, out_imag], axis=1)
    return stacked.reshape(stacked.shape[0], 2, stacked.shape[2], stacked.shape[3] * stacked.shape[4])

def inverse_planes(spectra, joint, y_cosine, y_sine):
    kept_y = y_cosine.shape[1]
    parts = spectra.reshape(spectra.shape[0], 2, spectra.shape[2], kept_y, spectra.shape[3] // kept_y)
    real_part = parts[:, 0]
    imag_part = parts[:, 1]
    out_real = jnp.einsum('xckm,yk->xcym', real_part, y_cosine, precision=HIGHEST) - jnp.einsum('xckm,yk->xcym', imag_part, y_sine, precision=HIGHEST)
    out_imag = jnp.einsum('xckm,yk->xcym', real_part, y_sine, precision=HIGHEST) + jnp.einsum('xckm,yk->xcym', imag_part, y_cosine, precision=HIGHEST)
    joined = jnp.concatenate([out_real, out_imag], axis=-1)
    joined = lax.optimization_barrier(joined.astype(jnp.bfloat16)).astype(jnp.float32)
    return jnp.einsum('xcyq,pq->xcyp', joined, joint.astype(jnp.float32), precision=HIGHEST)

def to_modes(spectra, x_cosine, x_sine):
    real_part = spectra[:, 0]
    imag_part = spectra[:, 1]
    out_real = jnp.einsum('xcm,xk->mck', real_part, x_cosine, precision=HIGHEST) + jnp.einsum('xcm,xk->mck', imag_part, x_sine, precision=HIGHEST)
    out_imag = jnp.einsum('xcm,xk->mck', imag_part, x_cosine, precision=HIGHEST) - jnp.einsum('xcm,xk->mck', real_part, x_sine, precision=HIGHEST)
    return jnp.stack([out_real, out_imag], axis=1)

def to_planes(mixed, x_cosine, x_sine):
    real_part = mixed[:, 0]
    imag_part = mixed[:, 1]
    out_real = jnp.einsum('mck,xk->xcm', real_part, x_cosine, precision=HIGHEST) - jnp.einsum('mck,xk->xcm', imag_part, x_sine, precision=HIGHEST)
    out_imag = jnp.einsum('mck,xk->xcm', real_part, x_sine, precision=HIGHEST) + jnp.einsum('mck,xk->xcm', imag_part, x_cosine, precision=HIGHEST)
    return jnp.stack([out_real, out_imag], axis=1)

def split_weight(spectral_weight):
    full = spectral_weight.astype(jnp.float32)
    return full.reshape(full.shape[0], 2, full.shape[2], full.shape[3] // full.shape[2], full.shape[2])

def mode_product(modes, spectral_weight):
    weight_parts = split_weight(spectral_weight)
    w_real = weight_parts[:, 0]
    w_imag = weight_parts[:, 1]
    m_real = modes[:, 0]
    m_imag = modes[:, 1]
    out_real = jnp.einsum('mik,miko->mok', m_real, w_real, precision=HIGHEST) - jnp.einsum('mik,miko->mok', m_imag, w_imag, precision=HIGHEST)
    out_imag = jnp.einsum('mik,miko->mok', m_real, w_imag, precision=HIGHEST) + jnp.einsum('mik,miko->mok', m_imag, w_real, precision=HIGHEST)
    return jnp.stack([out_real, out_imag], axis=1)

def mode_adjoint(dmodes, spectral_weight):
    weight_parts = split_weight(spectral_weight)
    w_real = weight_parts[:, 0]
    w_imag = weight_parts[:, 1]
    d_real = dmodes[:, 0]
    d_imag = dmodes[:, 1]
    out_real = jnp.einsum('mok,miko->mik', d_real, w_real, precision=HIGHEST) + jnp.einsum('mok,miko->mik', d_imag, w_imag, precision=HIGHEST)
    out_imag = jnp.einsum('mok,miko->mik', d_imag, w_real, precision=HIGHEST) - jnp.einsum('mok,miko->mik', d_real, w_imag, precision=HIGHEST)
    return jnp.stack([out_real, out_imag], axis=1)

def mode_gradient(modes, dmodes):
    m_real = modes[:, 0]
    m_imag = modes[:, 1]
    d_real = dmodes[:, 0]
    d_imag = dmodes[:, 1]
    out_real = jnp.einsum('mik,mok->miko', m_real, d_real, precision=HIGHEST) + jnp.einsum('mik,mok->miko', m_imag, d_imag, precision=HIGHEST)
    out_imag = jnp.einsum('mik,mok->miko', m_real, d_imag, precision=HIGHEST) - jnp.einsum('mik,mok->miko', m_imag, d_real, precision=HIGHEST)
    stacked = jnp.stack([out_real, out_imag], axis=1)
    return stacked.reshape(stacked.shape[0], 2, stacked.shape[2], stacked.shape[3] * stacked.shape[4])

def mode_scale(first_mode, mode_count):
    serial = first_mode + jnp.arange(mode_count, dtype=jnp.int32)
    weights = jnp.where(serial % KT == 0, 1.0, 2.0) / (NX * NY * NZ * NT)
    return weights[:, None, None, None]

def gelu_value(values):
    return 0.5 * values * (1.0 + jax.scipy.special.erf(values / math.sqrt(2.0)))

def gelu_slope(values):
    return 0.5 * (1.0 + jax.scipy.special.erf(values / math.sqrt(2.0))) + values * jnp.exp(-0.5 * values * values) / math.sqrt(2.0 * math.pi)

def reference(hidden_field, cotangent, spectral_weight, local_weight, local_bias):
    joint = joint_table()
    y_cosine, y_sine = axis_tables(jnp.arange(NY, dtype=jnp.int32), NY, KY)
    x_cosine, x_sine = axis_tables(jnp.arange(NX, dtype=jnp.int32), NX, KX)
    weight_full = local_weight.astype(jnp.float32)
    bias_full = local_bias.astype(jnp.float32)[None, :, None, None]

    def plane_spectra(plane):
        return forward_planes(plane[None].astype(jnp.float32), joint, y_cosine, y_sine)[0]
    spectra = lax.map(plane_spectra, hidden_field)
    modes = to_modes(spectra, x_cosine, x_sine)
    factor = mode_scale(0, KY * KZ * KT)
    mixed = mode_product(modes, spectral_weight) * factor
    back = to_planes(mixed, x_cosine, x_sine)

    def slope_of(plane, grad_plane, back_plane):
        values = plane[None].astype(jnp.float32)
        local_term = jnp.einsum('xiyp,io->xoyp', values, weight_full)
        pre = inverse_planes(back_plane[None], joint, y_cosine, y_sine) + local_term + bias_full
        slope = grad_plane[None].astype(jnp.float32) * gelu_slope(pre)
        slope_low = lax.optimization_barrier(slope.astype(jnp.bfloat16)).astype(jnp.float32)
        return (values, pre, slope, slope_low)

    def first_pass(items):
        values, pre, slope, slope_low = slope_of(items[0], items[1], items[2])
        result = gelu_value(pre).astype(jnp.bfloat16)[0]
        local_part = jnp.einsum('xiyp,xoyp->io', values, slope_low)
        bias_part = lax.optimization_barrier(jnp.sum(slope, axis=(0, 2, 3)))
        dspectra = forward_planes(slope_low, joint, y_cosine, y_sine)[0]
        return (result, local_part, bias_part, dspectra)
    output, local_parts, bias_parts, dspectra = lax.map(first_pass, (hidden_field, cotangent, back))
    grad_local = lax.optimization_barrier(jnp.sum(local_parts, axis=0))
    grad_bias = lax.optimization_barrier(jnp.sum(bias_parts, axis=0))
    dmodes = to_modes(dspectra, x_cosine, x_sine) * factor
    grad_spectral = mode_gradient(modes, dmodes)
    dback = to_planes(mode_adjoint(dmodes, spectral_weight), x_cosine, x_sine)

    def second_pass(items):
        values, pre, slope, slope_low = slope_of(items[0], items[1], items[2])
        total = inverse_planes(items[3][None], joint, y_cosine, y_sine) + jnp.einsum('xoyp,io->xiyp', slope_low, weight_full)
        return total.astype(jnp.bfloat16)[0]
    grad_field = lax.map(second_pass, (hidden_field, cotangent, back, dback))
    return (output, grad_field, grad_spectral, grad_local, grad_bias)
```

```python
import functools
import math

import jax
import jax.numpy as jnp
import ml_dtypes
import numpy as np
from jax import lax
from jax.experimental import pallas as pl
from jax.experimental.pallas import tpu as pltpu
from jax.sharding import PartitionSpec as P

NX, NY, NZ, NT = 128, 64, 64, 8
KX, KY, KZ, KT = 16, 16, 16, 4
C = 32
Q = KZ * KT
CELLS = NZ * NT
YB = 16
F32, BF16 = jnp.float32, jnp.bfloat16
HIGHEST = lax.Precision.HIGHEST
MIB = 1 << 20


def frequency(kept):
    serial = np.arange(kept)
    return np.where(serial < kept // 2, serial, serial - kept)


def angles(positions, length, kept):
    wound = (np.asarray(positions)[:, None] * frequency(kept)[None, :]) % length
    return 2.0 * math.pi / length * wound


def split2(table):
    high = table.astype(ml_dtypes.bfloat16)
    low = (table - high.astype(np.float64)).astype(ml_dtypes.bfloat16)
    return high, low


def zt_tables(modes_here):
    cells = np.arange(CELLS)
    depth, moment = cells // NT, cells % NT
    kept_z, kept_t = np.repeat(frequency(KZ), KT), np.tile(np.arange(KT), KZ)
    wound = (depth[:, None] * kept_z * NT + moment[:, None] * kept_t * NZ) % CELLS
    theta = 2.0 * math.pi / CELLS * wound
    cosine, sine = np.cos(theta), np.sin(theta)
    groups = Q // modes_here
    shape = (CELLS, groups, modes_here)
    cosine, sine = cosine.reshape(shape), sine.reshape(shape)
    first = np.stack([cosine, -sine], axis=2).reshape(CELLS, 2 * Q)
    second = np.stack([-sine, -cosine], axis=2).reshape(CELLS, 2 * Q)
    return np.concatenate([first, second], axis=1).astype(ml_dtypes.bfloat16)


def y_forward_table():
    theta = angles(np.arange(NY), NY, KY)
    table = np.concatenate([np.cos(theta), np.sin(theta)], axis=0).T
    high, low = split2(table)
    return np.concatenate([high, low], axis=0)


def y_inverse_table():
    theta = angles(np.arange(NY), NY, KY)
    table = np.concatenate([np.cos(theta), np.sin(theta)], axis=0)
    high, low = split2(table)
    return np.concatenate([high, high, low], axis=1)


def x_tables(planes, devices):
    theta = angles(np.arange(devices) * planes, NX, KX).T
    cosine, sine = np.cos(theta), np.sin(theta)
    forward = np.block([[cosine, sine], [-sine, cosine]]).astype(np.float32)
    turn = np.repeat(angles(np.arange(planes), NX, KX).T, C, axis=1)
    return (
        forward,
        np.ascontiguousarray(forward.T),
        np.cos(turn).astype(np.float32),
        np.sin(turn).astype(np.float32),
    )


def diagonal_mask():
    return (np.arange(KX * C)[None, :] // C == np.arange(KX)[:, None]).astype(np.float32)


def halves(value):
    high = value.astype(BF16)
    return high, (value - high.astype(F32)).astype(BF16)


def dot(left, right):
    return jnp.dot(left, right, preferred_element_type=F32)


def lane_total(value, step):
    span = value.shape[1] // 2
    while span >= step:
        value = value + pltpu.roll(value, span, 1)
        span //= 2
    return value


def y_forward(sums, y_table, gathered, first_row, lanes):
    count = sums.shape[0] // NY
    for pair in range(0, count, 2):
        one = sums[pair * NY : (pair + 1) * NY].astype(BF16)
        two = sums[(pair + 1) * NY : (pair + 2) * NY].astype(BF16)
        right = jnp.concatenate(
            [
                jnp.concatenate([one[:, : 2 * Q], two[:, : 2 * Q]], axis=1),
                jnp.concatenate([one[:, 2 * Q :], two[:, 2 * Q :]], axis=1),
            ],
            axis=0,
        )
        both = dot(y_table, right)
        out = both[:KY] + both[KY:]
        gathered[pl.ds(first_row + pair, KY, stride=lanes), :] = out[:, : 2 * Q]
        gathered[pl.ds(first_row + pair + 1, KY, stride=lanes), :] = out[:, 2 * Q :]


def send_layout(gathered, out_ref, lanes):
    for ky in range(KY):
        out_ref[ky * 2 * Q : (ky + 1) * 2 * Q, :] = gathered[ky * lanes : (ky + 1) * lanes, :].T


def forward_kernel(field, zt, y_table, out, gathered, *, lanes, block):
    plane, part = pl.program_id(0), pl.program_id(1)
    sums = dot(field[0].reshape(block * NY, CELLS), zt[...])
    y_forward(sums, y_table[...], gathered, plane * C + part * block, lanes)

    @pl.when((plane == pl.num_programs(0) - 1) & (part == pl.num_programs(1) - 1))
    def _():
        send_layout(gathered, out, lanes)


def forward_planes(field, zt, y_table):
    planes = field.shape[0]
    lanes, block = planes * C, 8
    return pl.pallas_call(
        functools.partial(forward_kernel, lanes=lanes, block=block),
        grid=(planes, C // block),
        in_specs=[
            pl.BlockSpec((1, block, NY, CELLS), lambda x, c: (x, c, 0, 0)),
            pl.BlockSpec(zt.shape, lambda x, c: (0, 0)),
            pl.BlockSpec(y_table.shape, lambda x, c: (0, 0)),
        ],
        out_specs=pl.BlockSpec((KY * 2 * Q, lanes), lambda x, c: (0, 0)),
        out_shape=jax.ShapeDtypeStruct((KY * 2 * Q, lanes), F32),
        scratch_shapes=[pltpu.VMEM((KY * lanes, 2 * Q), F32)],
        compiler_params=pltpu.CompilerParams(vmem_limit_bytes=32 * MIB),
        cost_estimate=pl.CostEstimate(flops=2 * 10**9, bytes_accessed=9 * MIB, transcendentals=0),
    )(field, zt, y_table)


QB = 8


def modes_of(received, q_count, devices, lanes, forward, cosine, sine):
    columns = []
    for q in range(q_count):
        parts = [
            received[pl.ds(ri * q_count + q, devices, stride=2 * q_count), :] for ri in range(2)
        ]
        columns.append(jnp.concatenate(parts, axis=0))
    right = jnp.concatenate(columns, axis=1) if lanes % 128 == 0 else None
    found = []
    if right is not None:
        summed = jnp.dot(forward, right, precision=HIGHEST, preferred_element_type=F32)
    for q in range(q_count):
        if right is not None:
            one = summed[:, q * lanes : (q + 1) * lanes]
        else:
            one = jnp.dot(forward, columns[q], precision=HIGHEST, preferred_element_type=F32)
        a_re, a_im = one[:KX], one[KX:]
        m_re = lane_total(a_re * cosine + a_im * sine, C)
        m_im = lane_total(a_im * cosine - a_re * sine, C)
        found.append((m_re, m_im))
    return found


def to_planes(mixed, out, q_count, devices, lanes, inverse, cosine, sine):
    turned = []
    for re, im in mixed:
        turned.append(
            jnp.concatenate([re * cosine - im * sine, re * sine + im * cosine], axis=0)
        )
    if lanes % 128 == 0:
        joined = jnp.concatenate(turned, axis=1)
        back = jnp.dot(inverse, joined, precision=HIGHEST, preferred_element_type=F32)
        backs = [back[:, q * lanes : (q + 1) * lanes] for q in range(q_count)]
    else:
        backs = [
            jnp.dot(inverse, one, precision=HIGHEST, preferred_element_type=F32) for one in turned
        ]
    for q in range(q_count):
        for ri in range(2):
            out[pl.ds(ri * q_count + q, devices, stride=2 * q_count), :] = backs[q][
                ri * devices : (ri + 1) * devices
            ]


def mode_factor(first, q):
    time_frequency = lax.rem(first + q, KT)
    return jnp.where(time_frequency == 0, 1.0, 2.0).astype(F32) / (NX * NY * NZ * NT)


def mix_kernel(
    received, weight, forward, inverse, cosine, sine, mask, out, modes_out, *, devices, lanes
):
    first = pl.program_id(0) * QB
    flat_in = received.reshape(devices * 2 * QB, lanes)
    flat_out = out.reshape(devices * 2 * QB, lanes)
    modes = modes_of(flat_in, QB, devices, lanes, forward[...], cosine[...], sine[...])
    mixed = []
    for q in range(QB):
        both = jnp.concatenate(modes[q], axis=0)
        modes_out[q] = both
        high, low = halves(both[:, :C])
        left = jnp.concatenate([high, low], axis=0)
        by_re, by_im = dot(left, weight[q, 0]), dot(left, weight[q, 1])
        by_re, by_im = by_re[: 2 * KX] + by_re[2 * KX :], by_im[: 2 * KX] + by_im[2 * KX :]
        factor = mode_factor(first, q)
        pieces = []
        for wide in (by_re[:KX] - by_im[KX:], by_im[:KX] + by_re[KX:]):
            kept = wide * mask[...]
            total = kept[:, :128]
            for column in range(128, KX * C, 128):
                total = total + kept[:, column : column + 128]
            pieces.append(lane_total(total, C)[:, :lanes] * factor)
        mixed.append(pieces)
    to_planes(mixed, flat_out, QB, devices, lanes, inverse[...], cosine[...], sine[...])


def whole(array):
    return pl.BlockSpec(array.shape, lambda *_: (0,) * array.ndim)


def mode_specs(devices, modes_here, lanes):
    slab = pl.BlockSpec((devices, 2, QB, lanes), lambda s: (0, 0, s, 0))
    weight = pl.BlockSpec((QB, 2, C, KX * C), lambda s: (s, 0, 0, 0))
    modes = pl.BlockSpec((QB, 2 * KX, lanes), lambda s: (s, 0, 0))
    return slab, weight, modes


def mix_modes(received, weight, tables):
    devices, _, modes_here, lanes = received.shape
    slab, weight_spec, modes = mode_specs(devices, modes_here, lanes)
    return pl.pallas_call(
        functools.partial(mix_kernel, devices=devices, lanes=lanes),
        grid=(modes_here // QB,),
        in_specs=[slab, weight_spec] + [whole(table) for table in tables],
        out_specs=[slab, modes],
        out_shape=[
            jax.ShapeDtypeStruct(received.shape, F32),
            jax.ShapeDtypeStruct((modes_here, 2 * KX, lanes), F32),
        ],
        compiler_params=pltpu.CompilerParams(vmem_limit_bytes=32 * MIB),
        cost_estimate=pl.CostEstimate(flops=10**9, bytes_accessed=5 * MIB, transcendentals=0),
    )(received, weight, *tables)


def spread(value, mask):
    if value.shape[1] < 128:
        value = jnp.concatenate([value] * (128 // value.shape[1]), axis=1)
    else:
        value = value[:, :128]
    return jnp.concatenate([value] * (KX * C // 128), axis=1) * mask


def adjoint_kernel(
    received, weight, forward, inverse, cosine, sine, mask, out, modes_out, *, devices, lanes
):
    first = pl.program_id(0) * QB
    flat_in = received.reshape(devices * 2 * QB, lanes)
    flat_out = out.reshape(devices * 2 * QB, lanes)
    modes = modes_of(flat_in, QB, devices, lanes, forward[...], cosine[...], sine[...])
    group = lax.broadcasted_iota(jnp.int32, (KX, 128), 1) // C
    odd = group % 2 == 1
    mixed = []
    for q in range(QB):
        factor = mode_factor(first, q)
        d_re, d_im = modes[q][0] * factor, modes[q][1] * factor
        modes_out[q] = jnp.concatenate([d_re, d_im], axis=0)
        wide = jnp.concatenate([spread(d_re, mask[...]), spread(d_im, mask[...])], axis=0)
        high, low = halves(wide)
        left = jnp.concatenate([high, low], axis=0)
        right = jnp.concatenate([weight[q, 0], weight[q, 1]] * 2, axis=0)
        product = lax.dot_general(
            left, right, (((1,), (1,)), ((), ())), preferred_element_type=F32
        )
        product = product[: 2 * KX] + product[2 * KX :]
        re = product[:KX] + pltpu.roll(product[KX:], 128 - C, 1)
        im = product[KX:] - pltpu.roll(product[:KX], 128 - C, 1)
        re = jnp.where(odd, pltpu.roll(re, C, 1), re)
        im = jnp.where(odd, pltpu.roll(im, C, 1), im)
        mixed.append((re[:, :lanes], im[:, :lanes]))
    to_planes(mixed, flat_out, QB, devices, lanes, inverse[...], cosine[...], sine[...])


def adjoint_modes(received, weight, tables):
    devices, _, modes_here, lanes = received.shape
    slab, weight_spec, modes = mode_specs(devices, modes_here, lanes)
    return pl.pallas_call(
        functools.partial(adjoint_kernel, devices=devices, lanes=lanes),
        grid=(modes_here // QB,),
        in_specs=[slab, weight_spec] + [whole(table) for table in tables],
        out_specs=[slab, modes],
        out_shape=[
            jax.ShapeDtypeStruct(received.shape, F32),
            jax.ShapeDtypeStruct((modes_here, 2 * KX, lanes), F32),
        ],
        compiler_params=pltpu.CompilerParams(vmem_limit_bytes=32 * MIB),
        cost_estimate=pl.CostEstimate(flops=10**9, bytes_accessed=5 * MIB, transcendentals=0),
    )(received, weight, *tables)


def gradient_kernel(modes, dmodes, mask, out):
    for q in range(QB):
        left = modes[q][:, :C]
        l_high, l_low = halves(left)
        left = jnp.concatenate([l_high, l_high, l_low], axis=0)
        d_re, d_im = spread(dmodes[q, :KX], mask[...]), spread(dmodes[q, KX:], mask[...])
        for part, rows in ((0, (d_re, d_im)), (1, (d_im, -d_re))):
            high, low = halves(jnp.concatenate(rows, axis=0))
            right = jnp.concatenate([high, low, high], axis=0)
            out[q, part] = lax.dot_general(
                left, right, (((0,), (0,)), ((), ())), preferred_element_type=F32
            )


def mode_gradient(modes, dmodes, mask):
    modes_here, _, lanes = modes.shape
    spec = pl.BlockSpec((QB, 2 * KX, lanes), lambda s: (s, 0, 0))
    return pl.pallas_call(
        gradient_kernel,
        grid=(modes_here // QB,),
        in_specs=[spec, spec, whole(mask)],
        out_specs=pl.BlockSpec((QB, 2, C, KX * C), lambda s: (s, 0, 0, 0)),
        out_shape=jax.ShapeDtypeStruct((modes_here, 2, C, KX * C), F32),
        compiler_params=pltpu.CompilerParams(vmem_limit_bytes=32 * MIB),
        cost_estimate=pl.CostEstimate(flops=10**8, bytes_accessed=5 * MIB, transcendentals=0),
    )(modes, dmodes, mask)


def planes_layout(back, gathered, lanes):
    for ky in range(KY):
        gathered[ky * lanes : (ky + 1) * lanes, :] = back[ky * 2 * Q : (ky + 1) * 2 * Q, :].T


def y_inverse(gathered, y_table, inverse_y, plane, lanes):
    for c in range(0, C, 2):
        row = plane * C + c
        pair = jnp.concatenate(
            [
                gathered[pl.ds(row, KY, stride=lanes), :],
                gathered[pl.ds(row + 1, KY, stride=lanes), :],
            ],
            axis=1,
        )
        high, low = halves(pair)
        both = dot(y_table, jnp.concatenate([high, low, high], axis=0)).astype(BF16)
        for k in range(2):
            columns = slice(k * 2 * Q, (k + 1) * 2 * Q)
            inverse_y[c + k, :, : 2 * Q] = both[:NY, columns]
            inverse_y[c + k, :, 2 * Q :] = both[NY:, columns]


def middle_kernel(
    back,
    field,
    cotangent,
    local,
    bias,
    zt,
    zt_turned,
    y_back,
    y_table,
    out,
    slope_out,
    spectra,
    local_grad,
    bias_grad,
    gathered,
    inverse_y,
    pre,
    sums,
    collected,
    *,
    lanes,
):
    plane, part = pl.program_id(0), pl.program_id(1)
    rows = C * YB
    first_step = (plane == 0) & (part == 0)
    last_step = (plane == pl.num_programs(0) - 1) & (part == pl.num_programs(1) - 1)

    @pl.when(first_step)
    def _():
        planes_layout(back, gathered, lanes)
        local_grad[...] = jnp.zeros_like(local_grad)
        bias_grad[...] = jnp.zeros_like(bias_grad)

    @pl.when(part == 0)
    def _():
        y_inverse(gathered, y_back[...], inverse_y, plane, lanes)

    y_rows = pl.ds(pl.multiple_of(part * YB, YB), YB)
    values = field[0].reshape(rows, CELLS)
    own = inverse_y[:, y_rows, :].reshape(rows, 4 * Q)
    pre[...] = dot(local[...], values) + dot(own, zt_turned[...])

    chunk = 2
    half_root = 1.0 / math.sqrt(2.0)

    def pointwise(step, _):
        c = step * chunk
        r = pl.ds(pl.multiple_of(c * YB, chunk * YB), chunk * YB)
        v = pre[r, :] + bias[r, :]
        grade = cotangent[0, pl.ds(c, chunk)].reshape(chunk * YB, CELLS).astype(F32)
        normal = 0.5 + 0.5 * lax.erf(v * half_root)
        result = v * normal
        slope = grade * (normal + v * (jnp.exp(-0.5 * v * v) * (1.0 / math.sqrt(2.0 * math.pi))))
        out[0, pl.ds(c, chunk)] = result.astype(BF16).reshape(chunk, YB, CELLS)
        slope_out[0, pl.ds(c, chunk)] = slope.astype(BF16).reshape(chunk, YB, CELLS)
        folded = slope[:, :128]
        for column in range(128, CELLS, 128):
            folded = folded + slope[:, column : column + 128]
        bias_grad[r, :] += folded
        return 0

    lax.fori_loop(0, C // chunk, pointwise, 0, unroll=False)

    low = slope_out[0].reshape(rows, CELLS)
    sums[:, y_rows, :] = dot(low, zt[...]).reshape(C, YB, 4 * Q)
    local_grad[...] += lax.dot_general(
        values, low, (((1,), (1,)), ((), ())), preferred_element_type=F32
    )

    @pl.when(part == pl.num_programs(1) - 1)
    def _():
        y_forward(sums.reshape(C * NY, 4 * Q), y_table[...], collected, plane * C, lanes)

    @pl.when(last_step)
    def _():
        send_layout(collected, spectra, lanes)


def middle(back, field, cotangent, local, bias, zt, zt_turned, y_back, y_table):
    planes = field.shape[0]
    lanes, rows = planes * C, C * YB
    block = pl.BlockSpec((1, C, YB, CELLS), lambda x, y: (x, 0, y, 0))
    return pl.pallas_call(
        functools.partial(middle_kernel, lanes=lanes),
        grid=(planes, NY // YB),
        in_specs=[
            whole(back),
            block,
            block,
            whole(local),
            whole(bias),
            whole(zt),
            whole(zt_turned),
            whole(y_back),
            whole(y_table),
        ],
        out_specs=[
            block,
            block,
            pl.BlockSpec((KY * 2 * Q, lanes), lambda x, y: (0, 0)),
            pl.BlockSpec((rows, rows), lambda x, y: (0, 0)),
            pl.BlockSpec((rows, 128), lambda x, y: (0, 0)),
        ],
        out_shape=[
            jax.ShapeDtypeStruct(field.shape, BF16),
            jax.ShapeDtypeStruct(field.shape, BF16),
            jax.ShapeDtypeStruct((KY * 2 * Q, lanes), F32),
            jax.ShapeDtypeStruct((rows, rows), F32),
            jax.ShapeDtypeStruct((rows, 128), F32),
        ],
        scratch_shapes=[
            pltpu.VMEM((KY * lanes, 2 * Q), F32),
            pltpu.VMEM((C, NY, 4 * Q), BF16),
            pltpu.VMEM((rows, CELLS), F32),
            pltpu.VMEM((C, NY, 4 * Q), F32),
            pltpu.VMEM((KY * lanes, 2 * Q), F32),
        ],
        compiler_params=pltpu.CompilerParams(vmem_limit_bytes=48 * MIB),
        cost_estimate=pl.CostEstimate(
            flops=13 * 10**9, bytes_accessed=34 * MIB, transcendentals=8 * 10**6
        ),
    )(back, field, cotangent, local, bias, zt, zt_turned, y_back, y_table)


def last_kernel(back, slope, local, zt_turned, y_back, out, gathered, inverse_y, *, lanes):
    plane, part = pl.program_id(0), pl.program_id(1)
    rows = C * YB

    @pl.when((plane == 0) & (part == 0))
    def _():
        planes_layout(back, gathered, lanes)

    @pl.when(part == 0)
    def _():
        y_inverse(gathered, y_back[...], inverse_y, plane, lanes)

    y_rows = pl.ds(pl.multiple_of(part * YB, YB), YB)
    low = slope[0].reshape(rows, CELLS)
    own = inverse_y[:, y_rows, :].reshape(rows, 4 * Q)
    total = dot(local[...], low) + dot(own, zt_turned[...])
    out[0] = total.astype(BF16).reshape(C, YB, CELLS)


def last(back, slope, local, zt_turned, y_back):
    planes = slope.shape[0]
    lanes = planes * C
    block = pl.BlockSpec((1, C, YB, CELLS), lambda x, y: (x, 0, y, 0))
    return pl.pallas_call(
        functools.partial(last_kernel, lanes=lanes),
        grid=(planes, NY // YB),
        in_specs=[whole(back), block, whole(local), whole(zt_turned), whole(y_back)],
        out_specs=block,
        out_shape=jax.ShapeDtypeStruct(slope.shape, BF16),
        scratch_shapes=[
            pltpu.VMEM((KY * lanes, 2 * Q), F32),
            pltpu.VMEM((C, NY, 4 * Q), BF16),
        ],
        compiler_params=pltpu.CompilerParams(vmem_limit_bytes=32 * MIB),
        cost_estimate=pl.CostEstimate(
            flops=6 * 10**9, bytes_accessed=17 * MIB, transcendentals=0
        ),
    )(back, slope, local, zt_turned, y_back)


def on_device(hidden_field, cotangent, spectral_weight, local_weight, local_bias):
    planes, modes_here = hidden_field.shape[0], spectral_weight.shape[0]
    devices = lax.axis_size("gx")
    lanes = planes * C
    zt_host = zt_tables(modes_here)
    zt, zt_turned = jnp.asarray(zt_host), jnp.asarray(np.ascontiguousarray(zt_host.T))
    y_table, y_back = jnp.asarray(y_forward_table()), jnp.asarray(y_inverse_table())
    mask = jnp.asarray(diagonal_mask())
    tables = [jnp.asarray(table) for table in x_tables(planes, devices)] + [mask]

    eye = jnp.eye(YB, dtype=BF16)
    rows = C * YB
    local_back = (local_weight[:, None, :, None] * eye[None, :, None, :]).reshape(rows, rows)
    local_here = (local_weight.T[:, None, :, None] * eye[None, :, None, :]).reshape(rows, rows)
    bias = jnp.repeat(local_bias, YB)[:, None]

    def exchange(value):
        return lax.all_to_all(value, "gx", split_axis=0, concat_axis=0, tiled=True)

    def to_owner(spectra):
        return exchange(spectra.reshape(devices, 2, modes_here, lanes))

    def to_slabs(back):
        return exchange(back).reshape(KY * 2 * Q, lanes)

    spectra = forward_planes(hidden_field, zt, y_table)
    back, modes = mix_modes(to_owner(spectra), spectral_weight, tables)
    output, slope, dspectra, local_part, bias_part = middle(
        to_slabs(back), hidden_field, cotangent, local_here, bias, zt, zt_turned, y_back, y_table
    )
    dback, dmodes = adjoint_modes(to_owner(dspectra), spectral_weight, tables)
    grad_spectral = mode_gradient(modes, dmodes, mask)
    local_sum = jnp.einsum("iyoy->io", local_part.reshape(C, YB, C, YB))
    bias_sum = jnp.sum(bias_part.reshape(C, YB * 128), axis=1)
    partial = jnp.concatenate([local_sum.reshape(C * C // 128, 128), jnp.tile(bias_sum, 4)[None]])
    total = jnp.sum(lax.all_gather(partial, "gx"), axis=0)
    grad_local = total[: C * C // 128].reshape(C, C)
    grad_bias = total[C * C // 128, :C]
    grad_field = last(to_slabs(dback), slope, local_back, zt_turned, y_back)
    return (output, grad_field, grad_spectral, grad_local, grad_bias)


def solution(mesh):
    placed = (
        P(("groups", "gx"), None, None, None),
        P(("groups", "gx"), None, None, None),
        P("gx", None, None, None),
        P(),
        P(),
    )
    return jax.shard_map(
        on_device,
        mesh=mesh,
        in_specs=placed,
        out_specs=(
            P(("groups", "gx"), None, None, None),
            P(("groups", "gx"), None, None, None),
            P("gx", "groups", None, None),
            P("groups", None),
            P("groups"),
        ),
        check_vma=False,
    )
```

```python
import functools
import math

import jax
import jax.numpy as jnp
import ml_dtypes
import numpy as np
from jax import lax
from jax.experimental import pallas as pl
from jax.experimental.pallas import tpu as pltpu
from jax.sharding import PartitionSpec as P

NX, NY, NZ, NT = 128, 64, 64, 8
KX, KY, KZ, KT = 16, 16, 16, 4
C = 32
Q = KZ * KT
CELLS = NZ * NT
YB = 16
F32, BF16 = jnp.float32, jnp.bfloat16
HIGHEST = lax.Precision.HIGHEST
MIB = 1 << 20


def frequency(kept):
    serial = np.arange(kept)
    return np.where(serial < kept // 2, serial, serial - kept)


def angles(positions, length, kept):
    wound = (np.asarray(positions)[:, None] * frequency(kept)[None, :]) % length
    return 2.0 * math.pi / length * wound


def split2(table):
    high = table.astype(ml_dtypes.bfloat16)
    low = (table - high.astype(np.float64)).astype(ml_dtypes.bfloat16)
    return high, low


def zt_tables(modes_here):
    cells = np.arange(CELLS)
    depth, moment = cells // NT, cells % NT
    kept_z, kept_t = np.repeat(frequency(KZ), KT), np.tile(np.arange(KT), KZ)
    wound = (depth[:, None] * kept_z * NT + moment[:, None] * kept_t * NZ) % CELLS
    theta = 2.0 * math.pi / CELLS * wound
    cosine, sine = np.cos(theta), np.sin(theta)
    groups = Q // modes_here
    shape = (CELLS, groups, modes_here)
    cosine, sine = cosine.reshape(shape), sine.reshape(shape)
    first = np.stack([cosine, -sine], axis=2).reshape(CELLS, 2 * Q)
    second = np.stack([-sine, -cosine], axis=2).reshape(CELLS, 2 * Q)
    return np.concatenate([first, second], axis=1).astype(ml_dtypes.bfloat16)


def y_forward_table():
    theta = angles(np.arange(NY), NY, KY)
    table = np.concatenate([np.cos(theta), np.sin(theta)], axis=0).T
    high, low = split2(table)
    return np.concatenate([high, low], axis=0)


def y_inverse_table():
    theta = angles(np.arange(NY), NY, KY)
    table = np.concatenate([np.cos(theta), np.sin(theta)], axis=0)
    high, low = split2(table)
    return np.concatenate([high, high, low], axis=1)


def x_tables(planes, devices):
    theta = angles(np.arange(devices) * planes, NX, KX).T
    cosine, sine = np.cos(theta), np.sin(theta)
    forward = np.block([[cosine, sine], [-sine, cosine]]).astype(np.float32)
    turn = np.repeat(angles(np.arange(planes), NX, KX).T, C, axis=1)
    return (
        forward,
        np.ascontiguousarray(forward.T),
        np.cos(turn).astype(np.float32),
        np.sin(turn).astype(np.float32),
    )


def diagonal_mask():
    return (np.arange(KX * C)[None, :] // C == np.arange(KX)[:, None]).astype(np.float32)


def halves(value):
    high = value.astype(BF16)
    return high, (value - high.astype(F32)).astype(BF16)


def dot(left, right):
    return jnp.dot(left, right, preferred_element_type=F32)


def lane_total(value, step):
    span = value.shape[1] // 2
    while span >= step:
        value = value + pltpu.roll(value, span, 1)
        span //= 2
    return value


def y_forward(sums, y_table, gathered, first_row, lanes):
    count = sums.shape[0] // NY
    for pair in range(0, count, 2):
        one = sums[pair * NY : (pair + 1) * NY].astype(BF16)
        two = sums[(pair + 1) * NY : (pair + 2) * NY].astype(BF16)
        right = jnp.concatenate(
            [
                jnp.concatenate([one[:, : 2 * Q], two[:, : 2 * Q]], axis=1),
                jnp.concatenate([one[:, 2 * Q :], two[:, 2 * Q :]], axis=1),
            ],
            axis=0,
        )
        both = dot(y_table, right)
        out = both[:KY] + both[KY:]
        gathered[pl.ds(first_row + pair, KY, stride=lanes), :] = out[:, : 2 * Q]
        gathered[pl.ds(first_row + pair + 1, KY, stride=lanes), :] = out[:, 2 * Q :]


def send_layout(gathered, out_ref, lanes):
    for ky in range(KY):
        out_ref[ky * 2 * Q : (ky + 1) * 2 * Q, :] = gathered[ky * lanes : (ky + 1) * lanes, :].T


def forward_kernel(field, zt, y_table, out, gathered, *, lanes, block, group):
    plane, part = pl.program_id(0), pl.program_id(1)
    for c in range(0, block, group):
        sums = dot(field[0, c : c + group].reshape(group * NY, CELLS), zt[...])
        y_forward(sums, y_table[...], gathered, plane * C + part * block + c, lanes)

    @pl.when((plane == pl.num_programs(0) - 1) & (part == pl.num_programs(1) - 1))
    def _():
        send_layout(gathered, out, lanes)


def forward_planes(field, zt, y_table, block=C, group=16):
    planes = field.shape[0]
    lanes = planes * C
    return pl.pallas_call(
        functools.partial(forward_kernel, lanes=lanes, block=block, group=group),
        grid=(planes, C // block),
        in_specs=[
            pl.BlockSpec((1, block, NY, CELLS), lambda x, c: (x, c, 0, 0)),
            whole(zt),
            whole(y_table),
        ],
        out_specs=pl.BlockSpec((KY * 2 * Q, lanes), lambda x, c: (0, 0)),
        out_shape=jax.ShapeDtypeStruct((KY * 2 * Q, lanes), F32),
        scratch_shapes=[pltpu.VMEM((KY * lanes, 2 * Q), F32)],
        compiler_params=pltpu.CompilerParams(vmem_limit_bytes=56 * MIB),
        cost_estimate=pl.CostEstimate(flops=2 * 10**9, bytes_accessed=9 * MIB, transcendentals=0),
    )(field, zt, y_table)


QB = 8


def modes_of(received, q_count, devices, lanes, forward, cosine, sine):
    columns = []
    for q in range(q_count):
        parts = [
            received[pl.ds(ri * q_count + q, devices, stride=2 * q_count), :] for ri in range(2)
        ]
        columns.append(jnp.concatenate(parts, axis=0))
    right = jnp.concatenate(columns, axis=1) if lanes % 128 == 0 else None
    found = []
    if right is not None:
        summed = jnp.dot(forward, right, precision=HIGHEST, preferred_element_type=F32)
    for q in range(q_count):
        if right is not None:
            one = summed[:, q * lanes : (q + 1) * lanes]
        else:
            one = jnp.dot(forward, columns[q], precision=HIGHEST, preferred_element_type=F32)
        a_re, a_im = one[:KX], one[KX:]
        m_re = lane_total(a_re * cosine + a_im * sine, C)
        m_im = lane_total(a_im * cosine - a_re * sine, C)
        found.append((m_re, m_im))
    return found


def to_planes(mixed, out, q_count, devices, lanes, inverse, cosine, sine):
    turned = []
    for re, im in mixed:
        turned.append(
            jnp.concatenate([re * cosine - im * sine, re * sine + im * cosine], axis=0)
        )
    if lanes % 128 == 0:
        joined = jnp.concatenate(turned, axis=1)
        back = jnp.dot(inverse, joined, precision=HIGHEST, preferred_element_type=F32)
        backs = [back[:, q * lanes : (q + 1) * lanes] for q in range(q_count)]
    else:
        backs = [
            jnp.dot(inverse, one, precision=HIGHEST, preferred_element_type=F32) for one in turned
        ]
    for q in range(q_count):
        for ri in range(2):
            out[pl.ds(ri * q_count + q, devices, stride=2 * q_count), :] = backs[q][
                ri * devices : (ri + 1) * devices
            ]


def mode_factor(first, q):
    time_frequency = lax.rem(first + q, KT)
    return jnp.where(time_frequency == 0, 1.0, 2.0).astype(F32) / (NX * NY * NZ * NT)


def mix_kernel(
    received, weight, forward, inverse, cosine, sine, mask, out, modes_out, *, devices, lanes
):
    first = pl.program_id(0) * QB
    flat_in = received.reshape(devices * 2 * QB, lanes)
    flat_out = out.reshape(devices * 2 * QB, lanes)
    modes = modes_of(flat_in, QB, devices, lanes, forward[...], cosine[...], sine[...])
    mixed = []
    for q in range(QB):
        both = jnp.concatenate(modes[q], axis=0)
        modes_out[q] = both
        high, low = halves(both[:, :C])
        left = jnp.concatenate([high, low], axis=0)
        by_re, by_im = dot(left, weight[q, 0]), dot(left, weight[q, 1])
        by_re, by_im = by_re[: 2 * KX] + by_re[2 * KX :], by_im[: 2 * KX] + by_im[2 * KX :]
        factor = mode_factor(first, q)
        pieces = []
        for wide in (by_re[:KX] - by_im[KX:], by_im[:KX] + by_re[KX:]):
            kept = wide * mask[...]
            total = kept[:, :128]
            for column in range(128, KX * C, 128):
                total = total + kept[:, column : column + 128]
            pieces.append(lane_total(total, C)[:, :lanes] * factor)
        mixed.append(pieces)
    to_planes(mixed, flat_out, QB, devices, lanes, inverse[...], cosine[...], sine[...])


def whole(array):
    return pl.BlockSpec(array.shape, lambda *_: (0,) * array.ndim)


def mode_specs(devices, modes_here, lanes):
    slab = pl.BlockSpec((devices, 2, QB, lanes), lambda s: (0, 0, s, 0))
    weight = pl.BlockSpec((QB, 2, C, KX * C), lambda s: (s, 0, 0, 0))
    modes = pl.BlockSpec((QB, 2 * KX, lanes), lambda s: (s, 0, 0))
    return slab, weight, modes


def mix_modes(received, weight, tables):
    devices, _, modes_here, lanes = received.shape
    slab, weight_spec, modes = mode_specs(devices, modes_here, lanes)
    return pl.pallas_call(
        functools.partial(mix_kernel, devices=devices, lanes=lanes),
        grid=(modes_here // QB,),
        in_specs=[slab, weight_spec] + [whole(table) for table in tables],
        out_specs=[slab, modes],
        out_shape=[
            jax.ShapeDtypeStruct(received.shape, F32),
            jax.ShapeDtypeStruct((modes_here, 2 * KX, lanes), F32),
        ],
        compiler_params=pltpu.CompilerParams(vmem_limit_bytes=32 * MIB),
        cost_estimate=pl.CostEstimate(flops=10**9, bytes_accessed=5 * MIB, transcendentals=0),
    )(received, weight, *tables)


def spread(value, mask):
    if value.shape[1] < 128:
        value = jnp.concatenate([value] * (128 // value.shape[1]), axis=1)
    else:
        value = value[:, :128]
    return jnp.concatenate([value] * (KX * C // 128), axis=1) * mask


def adjoint_kernel(
    received, weight, forward, inverse, cosine, sine, mask, out, modes_out, *, devices, lanes
):
    first = pl.program_id(0) * QB
    flat_in = received.reshape(devices * 2 * QB, lanes)
    flat_out = out.reshape(devices * 2 * QB, lanes)
    modes = modes_of(flat_in, QB, devices, lanes, forward[...], cosine[...], sine[...])
    group = lax.broadcasted_iota(jnp.int32, (KX, 128), 1) // C
    odd = group % 2 == 1
    mixed = []
    for q in range(QB):
        factor = mode_factor(first, q)
        d_re, d_im = modes[q][0] * factor, modes[q][1] * factor
        modes_out[q] = jnp.concatenate([d_re, d_im], axis=0)
        wide = jnp.concatenate([spread(d_re, mask[...]), spread(d_im, mask[...])], axis=0)
        high, low = halves(wide)
        left = jnp.concatenate([high, low], axis=0)
        right = jnp.concatenate([weight[q, 0], weight[q, 1]] * 2, axis=0)
        product = lax.dot_general(
            left, right, (((1,), (1,)), ((), ())), preferred_element_type=F32
        )
        product = product[: 2 * KX] + product[2 * KX :]
        re = product[:KX] + pltpu.roll(product[KX:], 128 - C, 1)
        im = product[KX:] - pltpu.roll(product[:KX], 128 - C, 1)
        re = jnp.where(odd, pltpu.roll(re, C, 1), re)
        im = jnp.where(odd, pltpu.roll(im, C, 1), im)
        mixed.append((re[:, :lanes], im[:, :lanes]))
    to_planes(mixed, flat_out, QB, devices, lanes, inverse[...], cosine[...], sine[...])


def adjoint_modes(received, weight, tables):
    devices, _, modes_here, lanes = received.shape
    slab, weight_spec, modes = mode_specs(devices, modes_here, lanes)
    return pl.pallas_call(
        functools.partial(adjoint_kernel, devices=devices, lanes=lanes),
        grid=(modes_here // QB,),
        in_specs=[slab, weight_spec] + [whole(table) for table in tables],
        out_specs=[slab, modes],
        out_shape=[
            jax.ShapeDtypeStruct(received.shape, F32),
            jax.ShapeDtypeStruct((modes_here, 2 * KX, lanes), F32),
        ],
        compiler_params=pltpu.CompilerParams(vmem_limit_bytes=32 * MIB),
        cost_estimate=pl.CostEstimate(flops=10**9, bytes_accessed=5 * MIB, transcendentals=0),
    )(received, weight, *tables)


def gradient_kernel(modes, dmodes, mask, out):
    for q in range(QB):
        left = modes[q][:, :C]
        l_high, l_low = halves(left)
        left = jnp.concatenate([l_high, l_high, l_low], axis=0)
        d_re, d_im = spread(dmodes[q, :KX], mask[...]), spread(dmodes[q, KX:], mask[...])
        for part, rows in ((0, (d_re, d_im)), (1, (d_im, -d_re))):
            high, low = halves(jnp.concatenate(rows, axis=0))
            right = jnp.concatenate([high, low, high], axis=0)
            out[q, part] = lax.dot_general(
                left, right, (((0,), (0,)), ((), ())), preferred_element_type=F32
            )


def mode_gradient(modes, dmodes, mask):
    modes_here, _, lanes = modes.shape
    spec = pl.BlockSpec((QB, 2 * KX, lanes), lambda s: (s, 0, 0))
    return pl.pallas_call(
        gradient_kernel,
        grid=(modes_here // QB,),
        in_specs=[spec, spec, whole(mask)],
        out_specs=pl.BlockSpec((QB, 2, C, KX * C), lambda s: (s, 0, 0, 0)),
        out_shape=jax.ShapeDtypeStruct((modes_here, 2, C, KX * C), F32),
        compiler_params=pltpu.CompilerParams(vmem_limit_bytes=32 * MIB),
        cost_estimate=pl.CostEstimate(flops=10**8, bytes_accessed=5 * MIB, transcendentals=0),
    )(modes, dmodes, mask)


def planes_layout(back, gathered, lanes):
    for ky in range(KY):
        gathered[ky * lanes : (ky + 1) * lanes, :] = back[ky * 2 * Q : (ky + 1) * 2 * Q, :].T


def y_inverse(gathered, y_table, first_row, count, lanes):
    found = []
    for c in range(0, count, 2):
        row = first_row + c
        pair = jnp.concatenate(
            [
                gathered[pl.ds(row, KY, stride=lanes), :],
                gathered[pl.ds(row + 1, KY, stride=lanes), :],
            ],
            axis=1,
        )
        high, low = halves(pair)
        both = dot(y_table, jnp.concatenate([high, low, high], axis=0)).astype(BF16)
        for k in range(2):
            columns = slice(k * 2 * Q, (k + 1) * 2 * Q)
            found.append(jnp.concatenate([both[:NY, columns], both[NY:, columns]], axis=1))
    return jnp.concatenate(found, axis=0)


def local_kernel(field, local, bias, out):
    rows = C * YB
    total = dot(local[...], field[0].reshape(rows, CELLS)) + bias[...]
    out[0] = total.astype(BF16).reshape(C, YB, CELLS)


def local_term(field, local, bias):
    block = pl.BlockSpec((1, C, YB, CELLS), lambda x, y: (x, 0, y, 0))
    return pl.pallas_call(
        local_kernel,
        grid=(field.shape[0], NY // YB),
        in_specs=[block, whole(local), whole(bias)],
        out_specs=block,
        out_shape=jax.ShapeDtypeStruct(field.shape, BF16),
        compiler_params=pltpu.CompilerParams(vmem_limit_bytes=32 * MIB),
        cost_estimate=pl.CostEstimate(flops=8 * 10**9, bytes_accessed=25 * MIB, transcendentals=0),
    )(field, local, bias)


def middle_kernel(
    back,
    early,
    cotangent,
    zt,
    zt_turned,
    y_back,
    y_table,
    out,
    slope_out,
    spectra,
    bias_grad,
    gathered,
    collected,
    *,
    lanes,
    block,
    group,
):
    plane, part = pl.program_id(0), pl.program_id(1)
    first_step = (plane == 0) & (part == 0)
    last_step = (plane == pl.num_programs(0) - 1) & (part == pl.num_programs(1) - 1)

    @pl.when(first_step)
    def _():
        planes_layout(back, gathered, lanes)
        bias_grad[...] = jnp.zeros_like(bias_grad)

    half_root = 1.0 / math.sqrt(2.0)
    for g in range(0, block, group):
        first_row = plane * C + part * block + g
        own = y_inverse(gathered, y_back[...], first_row, group, lanes)
        pre = dot(own, zt_turned[...])
        low = []
        for c in range(group):
            v = pre[c * NY : (c + 1) * NY] + early[0, g + c].astype(F32)
            grade = cotangent[0, g + c].astype(F32)
            normal = 0.5 + 0.5 * lax.erf(v * half_root)
            out[0, g + c] = (v * normal).astype(BF16)
            bell = jnp.exp(-0.5 * v * v) * (1.0 / math.sqrt(2.0 * math.pi))
            slope = grade * (normal + v * bell)
            low.append(slope.astype(BF16))
            slope_out[0, g + c] = low[-1]
            folded = slope[:, :128]
            for column in range(128, CELLS, 128):
                folded = folded + slope[:, column : column + 128]
            total = folded[:8]
            for row in range(8, NY, 8):
                total = total + folded[row : row + 8]
            r = pl.ds(pl.multiple_of((part * block + g + c) * 8, 8), 8)
            bias_grad[r, :] += total
        sums = dot(jnp.concatenate(low, axis=0), zt[...])
        y_forward(sums, y_table[...], collected, first_row, lanes)

    @pl.when(last_step)
    def _():
        send_layout(collected, spectra, lanes)


def middle(back, early, cotangent, zt, zt_turned, y_back, y_table, block=C, group=16):
    planes = cotangent.shape[0]
    lanes = planes * C
    spec = pl.BlockSpec((1, block, NY, CELLS), lambda x, c: (x, c, 0, 0))
    return pl.pallas_call(
        functools.partial(middle_kernel, lanes=lanes, block=block, group=group),
        grid=(planes, C // block),
        in_specs=[
            whole(back),
            spec,
            spec,
            whole(zt),
            whole(zt_turned),
            whole(y_back),
            whole(y_table),
        ],
        out_specs=[
            spec,
            spec,
            pl.BlockSpec((KY * 2 * Q, lanes), lambda x, c: (0, 0)),
            pl.BlockSpec((C * 8, 128), lambda x, c: (0, 0)),
        ],
        out_shape=[
            jax.ShapeDtypeStruct(cotangent.shape, BF16),
            jax.ShapeDtypeStruct(cotangent.shape, BF16),
            jax.ShapeDtypeStruct((KY * 2 * Q, lanes), F32),
            jax.ShapeDtypeStruct((C * 8, 128), F32),
        ],
        scratch_shapes=[
            pltpu.VMEM((KY * lanes, 2 * Q), F32),
            pltpu.VMEM((KY * lanes, 2 * Q), F32),
        ],
        compiler_params=pltpu.CompilerParams(vmem_limit_bytes=56 * MIB),
        cost_estimate=pl.CostEstimate(
            flops=5 * 10**9, bytes_accessed=42 * MIB, transcendentals=8 * 10**6
        ),
    )(back, early, cotangent, zt, zt_turned, y_back, y_table)


def late_kernel(field, slope, local, out, local_grad):
    rows = C * YB

    @pl.when((pl.program_id(0) == 0) & (pl.program_id(1) == 0))
    def _():
        local_grad[...] = jnp.zeros_like(local_grad)

    values, low = field[0].reshape(rows, CELLS), slope[0].reshape(rows, CELLS)
    out[0] = dot(local[...], low).astype(BF16).reshape(C, YB, CELLS)
    local_grad[...] += lax.dot_general(
        values, low, (((1,), (1,)), ((), ())), preferred_element_type=F32
    )


def late_terms(field, slope, local):
    block = pl.BlockSpec((1, C, YB, CELLS), lambda x, y: (x, 0, y, 0))
    rows = C * YB
    return pl.pallas_call(
        late_kernel,
        grid=(field.shape[0], NY // YB),
        in_specs=[block, block, whole(local)],
        out_specs=[block, pl.BlockSpec((rows, rows), lambda x, y: (0, 0))],
        out_shape=[
            jax.ShapeDtypeStruct(field.shape, BF16),
            jax.ShapeDtypeStruct((rows, rows), F32),
        ],
        compiler_params=pltpu.CompilerParams(vmem_limit_bytes=32 * MIB),
        cost_estimate=pl.CostEstimate(flops=12 * 10**9, bytes_accessed=25 * MIB, transcendentals=0),
    )(field, slope, local)


def last_kernel(back, early, zt_turned, y_back, out, gathered, *, lanes, block, group):
    plane, part = pl.program_id(0), pl.program_id(1)

    @pl.when((plane == 0) & (part == 0))
    def _():
        planes_layout(back, gathered, lanes)

    for g in range(0, block, group):
        own = y_inverse(gathered, y_back[...], plane * C + part * block + g, group, lanes)
        total = dot(own, zt_turned[...]).reshape(group, NY, CELLS)
        out[0, g : g + group] = (total + early[0, g : g + group].astype(F32)).astype(BF16)


def last(back, early, zt_turned, y_back, block=C, group=16):
    planes = early.shape[0]
    lanes = planes * C
    spec = pl.BlockSpec((1, block, NY, CELLS), lambda x, c: (x, c, 0, 0))
    return pl.pallas_call(
        functools.partial(last_kernel, lanes=lanes, block=block, group=group),
        grid=(planes, C // block),
        in_specs=[whole(back), spec, whole(zt_turned), whole(y_back)],
        out_specs=spec,
        out_shape=jax.ShapeDtypeStruct(early.shape, BF16),
        scratch_shapes=[pltpu.VMEM((KY * lanes, 2 * Q), F32)],
        compiler_params=pltpu.CompilerParams(vmem_limit_bytes=56 * MIB),
        cost_estimate=pl.CostEstimate(
            flops=2 * 10**9, bytes_accessed=17 * MIB, transcendentals=0
        ),
    )(back, early, zt_turned, y_back)


def on_device(hidden_field, cotangent, spectral_weight, local_weight, local_bias):
    planes, modes_here = hidden_field.shape[0], spectral_weight.shape[0]
    devices = lax.axis_size("gx")
    lanes = planes * C
    zt_host = zt_tables(modes_here)
    zt, zt_turned = jnp.asarray(zt_host), jnp.asarray(np.ascontiguousarray(zt_host.T))
    y_table, y_back = jnp.asarray(y_forward_table()), jnp.asarray(y_inverse_table())
    mask = jnp.asarray(diagonal_mask())
    tables = [jnp.asarray(table) for table in x_tables(planes, devices)] + [mask]

    eye = jnp.eye(YB, dtype=BF16)
    rows = C * YB
    local_back = (local_weight[:, None, :, None] * eye[None, :, None, :]).reshape(rows, rows)
    local_here = (local_weight.T[:, None, :, None] * eye[None, :, None, :]).reshape(rows, rows)
    bias = jnp.repeat(local_bias, YB)[:, None]

    def exchange(value):
        return lax.all_to_all(value, "gx", split_axis=0, concat_axis=0, tiled=True)

    def to_owner(spectra):
        return exchange(spectra.reshape(devices, 2, modes_here, lanes))

    def to_slabs(back):
        return exchange(back).reshape(KY * 2 * Q, lanes)

    spectra = forward_planes(hidden_field, zt, y_table)
    early = local_term(hidden_field, local_here, bias)
    back, modes = mix_modes(to_owner(spectra), spectral_weight, tables)
    output, slope, dspectra, bias_part = middle(
        to_slabs(back), early, cotangent, zt, zt_turned, y_back, y_table
    )
    late, local_part = late_terms(hidden_field, slope, local_back)
    dback, dmodes = adjoint_modes(to_owner(dspectra), spectral_weight, tables)
    grad_spectral = mode_gradient(modes, dmodes, mask)
    local_sum = jnp.einsum("iyoy->io", local_part.reshape(C, YB, C, YB))
    bias_sum = jnp.sum(bias_part.reshape(C, 8 * 128), axis=1)
    partial = jnp.concatenate([local_sum.reshape(C * C // 128, 128), jnp.tile(bias_sum, 4)[None]])
    copies = jnp.broadcast_to(partial, (devices,) + partial.shape)
    total = jnp.sum(exchange(copies), axis=0)
    grad_local = total[: C * C // 128].reshape(C, C)
    grad_bias = total[C * C // 128, :C]
    grad_field = last(to_slabs(dback), late, zt_turned, y_back)
    return (output, grad_field, grad_spectral, grad_local, grad_bias)


def solution(mesh):
    placed = (
        P(("groups", "gx"), None, None, None),
        P(("groups", "gx"), None, None, None),
        P("gx", None, None, None),
        P(),
        P(),
    )
    return jax.shard_map(
        on_device,
        mesh=mesh,
        in_specs=placed,
        out_specs=(
            P(("groups", "gx"), None, None, None),
            P(("groups", "gx"), None, None, None),
            P("gx", "groups", None, None),
            P("groups", None),
            P("groups"),
        ),
        check_vma=False,
    )
```

```python
import functools
import math

import jax
import jax.numpy as jnp
import ml_dtypes
import numpy as np
from jax import lax
from jax.experimental import pallas as pl
from jax.experimental.pallas import tpu as pltpu
from jax.sharding import PartitionSpec as P

NX, NY, NZ, NT = 128, 64, 64, 8
KX, KY, KZ, KT = 16, 16, 16, 4
C = 32
Q = KZ * KT
CELLS = NZ * NT
YB = 16
F32, BF16 = jnp.float32, jnp.bfloat16
HIGHEST = lax.Precision.HIGHEST
MIB = 1 << 20


def frequency(kept):
    serial = np.arange(kept)
    return np.where(serial < kept // 2, serial, serial - kept)


def angles(positions, length, kept):
    wound = (np.asarray(positions)[:, None] * frequency(kept)[None, :]) % length
    return 2.0 * math.pi / length * wound


def split2(table):
    high = table.astype(ml_dtypes.bfloat16)
    low = (table - high.astype(np.float64)).astype(ml_dtypes.bfloat16)
    return high, low


def stacked(table):
    high, low = split2(table)
    return np.concatenate([high, high, low], axis=1)


def zt_tables(modes_here):
    cells = np.arange(CELLS)
    depth, moment = cells // NT, cells % NT
    kept_z, kept_t = np.repeat(frequency(KZ), KT), np.tile(np.arange(KT), KZ)
    wound = (depth[:, None] * kept_z * NT + moment[:, None] * kept_t * NZ) % CELLS
    theta = 2.0 * math.pi / CELLS * wound
    cosine, sine = np.cos(theta), np.sin(theta)
    groups = Q // modes_here
    shape = (CELLS, groups, modes_here)
    cosine, sine = cosine.reshape(shape), sine.reshape(shape)
    first = np.stack([cosine, -sine], axis=2).reshape(CELLS, 2 * Q)
    second = np.stack([-sine, -cosine], axis=2).reshape(CELLS, 2 * Q)
    return np.concatenate([first, second], axis=1).astype(ml_dtypes.bfloat16)


def y_forward_table():
    theta = angles(np.arange(NY), NY, KY)
    table = np.concatenate([np.cos(theta), np.sin(theta)], axis=0).T
    high, low = split2(table)
    return np.concatenate([high, low], axis=0)


def y_inverse_table():
    theta = angles(np.arange(NY), NY, KY)
    table = np.concatenate([np.cos(theta), np.sin(theta)], axis=0)
    return stacked(table)


def x_tables(planes, devices):
    theta = angles(np.arange(devices) * planes, NX, KX).T
    cosine, sine = np.cos(theta), np.sin(theta)
    forward = np.block([[cosine, sine], [-sine, cosine]])
    turn = np.repeat(angles(np.arange(planes), NX, KX).T, C, axis=1)
    return (
        stacked(forward),
        stacked(forward.T),
        np.cos(turn).astype(np.float32),
        np.sin(turn).astype(np.float32),
    )


def diagonal_mask():
    return (np.arange(KX * C)[None, :] // C == np.arange(KX)[:, None]).astype(np.float32)


def halves(value):
    high = value.astype(BF16)
    return high, (value - high.astype(F32)).astype(BF16)


def three(value):
    high, low = halves(value)
    return jnp.concatenate([high, low, high], axis=0)


def dot(left, right):
    return jnp.dot(left, right, preferred_element_type=F32)


def lane_total(value, step):
    span = value.shape[1] // 2
    while span >= step:
        value = value + pltpu.roll(value, span, 1)
        span //= 2
    return value


def y_forward(sums, y_table, gathered, first_row, lanes):
    count = sums.shape[0] // NY
    for pair in range(0, count, 2):
        one = sums[pair * NY : (pair + 1) * NY].astype(BF16)
        two = sums[(pair + 1) * NY : (pair + 2) * NY].astype(BF16)
        right = jnp.concatenate(
            [
                jnp.concatenate([one[:, : 2 * Q], two[:, : 2 * Q]], axis=1),
                jnp.concatenate([one[:, 2 * Q :], two[:, 2 * Q :]], axis=1),
            ],
            axis=0,
        )
        both = dot(y_table, right)
        out = both[:KY] + both[KY:]
        gathered[pl.ds(first_row + pair, KY, stride=lanes), :] = out[:, : 2 * Q]
        gathered[pl.ds(first_row + pair + 1, KY, stride=lanes), :] = out[:, 2 * Q :]


def send_layout(gathered, out_ref, lanes):
    for ky in range(KY):
        out_ref[ky * 2 * Q : (ky + 1) * 2 * Q, :] = gathered[ky * lanes : (ky + 1) * lanes, :].T


def forward_kernel(field, zt, y_table, out, gathered, *, lanes, block, group):
    plane, part = pl.program_id(0), pl.program_id(1)
    for c in range(0, block, group):
        sums = dot(field[0, c : c + group].reshape(group * NY, CELLS), zt[...])
        y_forward(sums, y_table[...], gathered, plane * C + part * block + c, lanes)

    @pl.when((plane == pl.num_programs(0) - 1) & (part == pl.num_programs(1) - 1))
    def _():
        send_layout(gathered, out, lanes)


def forward_planes(field, zt, y_table, block=C, group=16):
    planes = field.shape[0]
    lanes = planes * C
    return pl.pallas_call(
        functools.partial(forward_kernel, lanes=lanes, block=block, group=group),
        grid=(planes, C // block),
        in_specs=[
            pl.BlockSpec((1, block, NY, CELLS), lambda x, c: (x, c, 0, 0)),
            whole(zt),
            whole(y_table),
        ],
        out_specs=pl.BlockSpec((KY * 2 * Q, lanes), lambda x, c: (0, 0)),
        out_shape=jax.ShapeDtypeStruct((KY * 2 * Q, lanes), F32),
        scratch_shapes=[pltpu.VMEM((KY * lanes, 2 * Q), F32)],
        compiler_params=pltpu.CompilerParams(vmem_limit_bytes=56 * MIB),
        cost_estimate=pl.CostEstimate(flops=2 * 10**9, bytes_accessed=9 * MIB, transcendentals=0),
    )(field, zt, y_table)


Q_BLOCK = 16


def modes_of(received, q_count, devices, lanes, forward, cosine, sine):
    columns = []
    for q in range(q_count):
        parts = [
            received[pl.ds(ri * q_count + q, devices, stride=2 * q_count), :] for ri in range(2)
        ]
        columns.append(jnp.concatenate(parts, axis=0))
    right = jnp.concatenate(columns, axis=1) if lanes % 128 == 0 else None
    found = []
    if right is not None:
        summed = dot(forward, three(right))
    for q in range(q_count):
        if right is not None:
            one = summed[:, q * lanes : (q + 1) * lanes]
        else:
            one = dot(forward, three(columns[q]))
        a_re, a_im = one[:KX], one[KX:]
        m_re = lane_total(a_re * cosine + a_im * sine, C)
        m_im = lane_total(a_im * cosine - a_re * sine, C)
        found.append((m_re, m_im))
    return found


def to_planes(mixed, out, q_count, devices, lanes, inverse, cosine, sine):
    turned = []
    for re, im in mixed:
        turned.append(
            jnp.concatenate([re * cosine - im * sine, re * sine + im * cosine], axis=0)
        )
    if lanes % 128 == 0:
        joined = jnp.concatenate(turned, axis=1)
        back = dot(inverse, three(joined))
        backs = [back[:, q * lanes : (q + 1) * lanes] for q in range(q_count)]
    else:
        backs = [dot(inverse, three(one)) for one in turned]
    for q in range(q_count):
        for ri in range(2):
            out[pl.ds(ri * q_count + q, devices, stride=2 * q_count), :] = backs[q][
                ri * devices : (ri + 1) * devices
            ]


def mode_factor(first, q):
    time_frequency = lax.rem(first + q, KT)
    return jnp.where(time_frequency == 0, 1.0, 2.0).astype(F32) / (NX * NY * NZ * NT)


def beside(one, two):
    if one.shape[1] < 128:
        return jnp.concatenate([one, two], axis=1)
    lane = lax.broadcasted_iota(jnp.int32, one.shape, 1)
    return jnp.where(lane < C, one, two)[:, : 2 * C]


def mix_kernel(
    received, weight, forward, inverse, cosine, sine, mask, out, modes_out, *, devices, lanes
):
    q_block = weight.shape[0]
    first = pl.program_id(0) * q_block
    flat_in = received.reshape(devices * 2 * q_block, lanes)
    flat_out = out.reshape(devices * 2 * q_block, lanes)
    modes = modes_of(flat_in, q_block, devices, lanes, forward[...], cosine[...], sine[...])
    own_block = jnp.concatenate([mask[...]] * 2, axis=0)
    mixed = []
    for q in range(q_block):
        re, im = modes[q]
        modes_out[q] = jnp.concatenate([re, im], axis=0)
        high, low = halves(jnp.concatenate([beside(re, -im), beside(im, re)], axis=0))
        product = dot(jnp.concatenate([high, low], axis=0), weight[q].reshape(2 * C, KX * C))
        kept = (product[: 2 * KX] + product[2 * KX :]) * own_block
        total = kept[:, :128]
        for column in range(128, KX * C, 128):
            total = total + kept[:, column : column + 128]
        total = lane_total(total, C)[:, :lanes] * mode_factor(first, q)
        pieces = (total[:KX], total[KX:])
        mixed.append(pieces)
    to_planes(mixed, flat_out, q_block, devices, lanes, inverse[...], cosine[...], sine[...])


def whole(array):
    return pl.BlockSpec(array.shape, lambda *_: (0,) * array.ndim)


def mode_specs(devices, modes_here, lanes):
    q_block = min(Q_BLOCK, modes_here)
    slab = pl.BlockSpec((devices, 2, q_block, lanes), lambda s: (0, 0, s, 0))
    weight = pl.BlockSpec((q_block, 2, C, KX * C), lambda s: (s, 0, 0, 0))
    modes = pl.BlockSpec((q_block, 2 * KX, lanes), lambda s: (s, 0, 0))
    return slab, weight, modes


def mix_modes(received, weight, tables):
    devices, _, modes_here, lanes = received.shape
    slab, weight_spec, modes = mode_specs(devices, modes_here, lanes)
    return pl.pallas_call(
        functools.partial(mix_kernel, devices=devices, lanes=lanes),
        grid=(modes_here // min(Q_BLOCK, modes_here),),
        in_specs=[slab, weight_spec] + [whole(table) for table in tables],
        out_specs=[slab, modes],
        out_shape=[
            jax.ShapeDtypeStruct(received.shape, F32),
            jax.ShapeDtypeStruct((modes_here, 2 * KX, lanes), F32),
        ],
        compiler_params=pltpu.CompilerParams(vmem_limit_bytes=32 * MIB),
        cost_estimate=pl.CostEstimate(flops=10**9, bytes_accessed=5 * MIB, transcendentals=0),
    )(received, weight, *tables)


def spread(value, mask):
    if value.shape[1] < 128:
        value = jnp.concatenate([value] * (128 // value.shape[1]), axis=1)
    else:
        value = value[:, :128]
    return jnp.concatenate([value] * (KX * C // 128), axis=1) * mask


def adjoint_kernel(
    received, weight, forward, inverse, cosine, sine, mask, out, modes_out, *, devices, lanes
):
    q_block = weight.shape[0]
    first = pl.program_id(0) * q_block
    flat_in = received.reshape(devices * 2 * q_block, lanes)
    flat_out = out.reshape(devices * 2 * q_block, lanes)
    modes = modes_of(flat_in, q_block, devices, lanes, forward[...], cosine[...], sine[...])
    group = lax.broadcasted_iota(jnp.int32, (KX, 128), 1) // C
    odd = group % 2 == 1
    mixed = []
    for q in range(q_block):
        factor = mode_factor(first, q)
        d_re, d_im = modes[q][0] * factor, modes[q][1] * factor
        modes_out[q] = jnp.concatenate([d_re, d_im], axis=0)
        wide = jnp.concatenate([spread(d_re, mask[...]), spread(d_im, mask[...])], axis=0)
        high, low = halves(wide)
        left = jnp.concatenate([high, low], axis=0)
        right = jnp.concatenate([weight[q, 0], weight[q, 1]] * 2, axis=0)
        product = lax.dot_general(
            left, right, (((1,), (1,)), ((), ())), preferred_element_type=F32
        )
        product = product[: 2 * KX] + product[2 * KX :]
        re = product[:KX] + pltpu.roll(product[KX:], 128 - C, 1)
        im = product[KX:] - pltpu.roll(product[:KX], 128 - C, 1)
        re = jnp.where(odd, pltpu.roll(re, C, 1), re)
        im = jnp.where(odd, pltpu.roll(im, C, 1), im)
        mixed.append((re[:, :lanes], im[:, :lanes]))
    to_planes(mixed, flat_out, q_block, devices, lanes, inverse[...], cosine[...], sine[...])


def adjoint_modes(received, weight, tables):
    devices, _, modes_here, lanes = received.shape
    slab, weight_spec, modes = mode_specs(devices, modes_here, lanes)
    return pl.pallas_call(
        functools.partial(adjoint_kernel, devices=devices, lanes=lanes),
        grid=(modes_here // min(Q_BLOCK, modes_here),),
        in_specs=[slab, weight_spec] + [whole(table) for table in tables],
        out_specs=[slab, modes],
        out_shape=[
            jax.ShapeDtypeStruct(received.shape, F32),
            jax.ShapeDtypeStruct((modes_here, 2 * KX, lanes), F32),
        ],
        compiler_params=pltpu.CompilerParams(vmem_limit_bytes=32 * MIB),
        cost_estimate=pl.CostEstimate(flops=10**9, bytes_accessed=5 * MIB, transcendentals=0),
    )(received, weight, *tables)


def gradient_kernel(modes, dmodes, mask, out):
    for q in range(modes.shape[0]):
        left = modes[q][:, :C]
        l_high, l_low = halves(left)
        left = jnp.concatenate([l_high, l_high, l_low], axis=0)
        d_re, d_im = spread(dmodes[q, :KX], mask[...]), spread(dmodes[q, KX:], mask[...])
        for part, rows in ((0, (d_re, d_im)), (1, (d_im, -d_re))):
            high, low = halves(jnp.concatenate(rows, axis=0))
            right = jnp.concatenate([high, low, high], axis=0)
            out[q, part] = lax.dot_general(
                left, right, (((0,), (0,)), ((), ())), preferred_element_type=F32
            )


def mode_gradient(modes, dmodes, mask):
    modes_here, _, lanes = modes.shape
    q_block = min(Q_BLOCK, modes_here)
    spec = pl.BlockSpec((q_block, 2 * KX, lanes), lambda s: (s, 0, 0))
    return pl.pallas_call(
        gradient_kernel,
        grid=(modes_here // q_block,),
        in_specs=[spec, spec, whole(mask)],
        out_specs=pl.BlockSpec((q_block, 2, C, KX * C), lambda s: (s, 0, 0, 0)),
        out_shape=jax.ShapeDtypeStruct((modes_here, 2, C, KX * C), F32),
        compiler_params=pltpu.CompilerParams(vmem_limit_bytes=32 * MIB),
        cost_estimate=pl.CostEstimate(flops=10**8, bytes_accessed=5 * MIB, transcendentals=0),
    )(modes, dmodes, mask)


def planes_layout(back, gathered, lanes):
    for ky in range(KY):
        gathered[ky * lanes : (ky + 1) * lanes, :] = back[ky * 2 * Q : (ky + 1) * 2 * Q, :].T


def y_inverse(gathered, y_table, first_row, count, lanes):
    found = []
    for c in range(0, count, 2):
        row = first_row + c
        pair = jnp.concatenate(
            [
                gathered[pl.ds(row, KY, stride=lanes), :],
                gathered[pl.ds(row + 1, KY, stride=lanes), :],
            ],
            axis=1,
        )
        both = dot(y_table, three(pair)).astype(BF16)
        for k in range(2):
            columns = slice(k * 2 * Q, (k + 1) * 2 * Q)
            found.append(jnp.concatenate([both[:NY, columns], both[NY:, columns]], axis=1))
    return jnp.concatenate(found, axis=0)


def row_pick():
    return (np.arange(C * YB)[:, None] // YB == np.arange(C)[None, :]).astype(ml_dtypes.bfloat16)


def same_y():
    rows = np.arange(C * YB)
    return (rows[:, None] % YB == rows[None, :] % YB).astype(ml_dtypes.bfloat16)


def channel_map(weight, pick, same, out):
    rows = dot(pick, weight).astype(BF16)
    wide = lax.dot_general(rows, pick, (((1,), (1,)), ((), ())), preferred_element_type=F32)
    out[...] = wide.astype(BF16) * same


def local_kernel(field, weight, bias, pick, same, out, local):
    rows = C * YB

    @pl.when((pl.program_id(0) == 0) & (pl.program_id(1) == 0))
    def _():
        channel_map(weight[...], pick[...], same[...], local)

    for part in range(field.shape[2] // YB):
        y = slice(part * YB, (part + 1) * YB)
        total = dot(local[...], field[0, :, y].reshape(rows, CELLS)) + bias[...]
        out[0, :, y] = total.astype(BF16).reshape(C, YB, CELLS)


def local_term(field, weight, bias, pick, same, parts=1):
    block = pl.BlockSpec((1, C, NY // parts, CELLS), lambda x, y: (x, 0, y, 0))
    rows = C * YB
    return pl.pallas_call(
        local_kernel,
        grid=(field.shape[0], parts),
        in_specs=[block, whole(weight), whole(bias), whole(pick), whole(same)],
        out_specs=block,
        out_shape=jax.ShapeDtypeStruct(field.shape, BF16),
        scratch_shapes=[pltpu.VMEM((rows, rows), BF16)],
        compiler_params=pltpu.CompilerParams(vmem_limit_bytes=56 * MIB),
        cost_estimate=pl.CostEstimate(flops=4 * 10**9, bytes_accessed=17 * MIB, transcendentals=0),
    )(field, weight, bias, pick, same)


def late_kernel(slope, weight, pick, same, out, local):
    rows = C * YB

    @pl.when((pl.program_id(0) == 0) & (pl.program_id(1) == 0))
    def _():
        channel_map(weight[...], pick[...], same[...], local)

    for part in range(slope.shape[2] // YB):
        y = slice(part * YB, (part + 1) * YB)
        total = dot(local[...], slope[0, :, y].reshape(rows, CELLS))
        out[0, :, y] = total.astype(BF16).reshape(C, YB, CELLS)


def late_term(slope, weight, pick, same, parts=1):
    block = pl.BlockSpec((1, C, NY // parts, CELLS), lambda x, y: (x, 0, y, 0))
    rows = C * YB
    return pl.pallas_call(
        late_kernel,
        grid=(slope.shape[0], parts),
        in_specs=[block, whole(weight), whole(pick), whole(same)],
        out_specs=block,
        out_shape=jax.ShapeDtypeStruct(slope.shape, BF16),
        scratch_shapes=[pltpu.VMEM((rows, rows), BF16)],
        compiler_params=pltpu.CompilerParams(vmem_limit_bytes=56 * MIB),
        cost_estimate=pl.CostEstimate(flops=4 * 10**9, bytes_accessed=17 * MIB, transcendentals=0),
    )(slope, weight, pick, same)


def pointwise_kernel(field, slope, bias_part, pick, same, out, total):
    rows = C * YB
    first_step = (pl.program_id(0) == 0) & (pl.program_id(1) == 0)
    last_step = (pl.program_id(0) == pl.num_programs(0) - 1) & (
        pl.program_id(1) == pl.num_programs(1) - 1
    )

    @pl.when(first_step)
    def _():
        total[...] = jnp.zeros_like(total)

    for part in range(field.shape[2] // YB):
        y = slice(part * YB, (part + 1) * YB)
        total[...] += lax.dot_general(
            field[0, :, y].reshape(rows, CELLS),
            slope[0, :, y].reshape(rows, CELLS),
            (((1,), (1,)), ((), ())),
            preferred_element_type=F32,
        )

    @pl.when(last_step)
    def _():
        to_f32 = functools.partial(
            lax.dot_general, precision=HIGHEST, preferred_element_type=F32
        )
        chosen = pick[...].astype(F32)
        tiled = jnp.concatenate([chosen] * 4, axis=1)
        kept = total[...] * same[...].astype(F32)
        across = to_f32(kept, tiled, (((1,), (0,)), ((), ())))
        grads = to_f32(chosen, across, (((0,), (0,)), ((), ())))
        group = lax.broadcasted_iota(jnp.int32, (8, 128), 1) // C
        folded = jnp.zeros((8, 128), F32)
        for g in range(4):
            folded = jnp.where(group == g, grads[g * 8 : (g + 1) * 8], folded)
        out[:8, :] = folded
        lane_sums = to_f32(jnp.ones((8, 128), F32), bias_part[...], (((1,), (1,)), ((), ())))
        by_channel = (
            lax.broadcasted_iota(jnp.int32, (8 * C, 128), 0) // 8
            == lax.broadcasted_iota(jnp.int32, (8 * C, 128), 1)
        ).astype(F32)
        out[8:, :] = to_f32(lane_sums, by_channel, (((1,), (0,)), ((), ())))


def pointwise_gradient(field, slope, bias_part, pick, same, parts=1):
    block = pl.BlockSpec((1, C, NY // parts, CELLS), lambda x, y: (x, 0, y, 0))
    rows = C * YB
    return pl.pallas_call(
        pointwise_kernel,
        grid=(field.shape[0], parts),
        in_specs=[block, block, whole(bias_part), whole(pick), whole(same)],
        out_specs=pl.BlockSpec((16, 128), lambda x, y: (0, 0)),
        out_shape=jax.ShapeDtypeStruct((16, 128), F32),
        scratch_shapes=[pltpu.VMEM((rows, rows), F32)],
        compiler_params=pltpu.CompilerParams(vmem_limit_bytes=56 * MIB),
        cost_estimate=pl.CostEstimate(flops=4 * 10**9, bytes_accessed=17 * MIB, transcendentals=0),
    )(field, slope, bias_part, pick, same)


def middle_kernel(
    back,
    early,
    cotangent,
    zt,
    zt_turned,
    y_back,
    y_table,
    out,
    slope_out,
    spectra,
    bias_grad,
    gathered,
    collected,
    *,
    lanes,
    block,
    group,
):
    plane, part = pl.program_id(0), pl.program_id(1)
    first_step = (plane == 0) & (part == 0)
    last_step = (plane == pl.num_programs(0) - 1) & (part == pl.num_programs(1) - 1)

    @pl.when(first_step)
    def _():
        planes_layout(back, gathered, lanes)
        bias_grad[...] = jnp.zeros_like(bias_grad)

    half_root = 1.0 / math.sqrt(2.0)
    for g in range(0, block, group):
        first_row = plane * C + part * block + g
        own = y_inverse(gathered, y_back[...], first_row, group, lanes)
        pre = dot(own, zt_turned[...])
        low = []
        for c in range(group):
            v = pre[c * NY : (c + 1) * NY] + early[0, g + c].astype(F32)
            grade = cotangent[0, g + c].astype(F32)
            normal = 0.5 + 0.5 * lax.erf(v * half_root)
            out[0, g + c] = (v * normal).astype(BF16)
            bell = jnp.exp(-0.5 * v * v) * (1.0 / math.sqrt(2.0 * math.pi))
            slope = grade * (normal + v * bell)
            low.append(slope.astype(BF16))
            slope_out[0, g + c] = low[-1]
            folded = slope[:, :128]
            for column in range(128, CELLS, 128):
                folded = folded + slope[:, column : column + 128]
            total = folded[:8]
            for row in range(8, NY, 8):
                total = total + folded[row : row + 8]
            r = pl.ds(pl.multiple_of((part * block + g + c) * 8, 8), 8)
            bias_grad[r, :] += total
        sums = dot(jnp.concatenate(low, axis=0), zt[...])
        y_forward(sums, y_table[...], collected, first_row, lanes)

    @pl.when(last_step)
    def _():
        send_layout(collected, spectra, lanes)


def middle(back, early, cotangent, zt, zt_turned, y_back, y_table, block=C, group=16):
    planes = cotangent.shape[0]
    lanes = planes * C
    spec = pl.BlockSpec((1, block, NY, CELLS), lambda x, c: (x, c, 0, 0))
    return pl.pallas_call(
        functools.partial(middle_kernel, lanes=lanes, block=block, group=group),
        grid=(planes, C // block),
        in_specs=[
            whole(back),
            spec,
            spec,
            whole(zt),
            whole(zt_turned),
            whole(y_back),
            whole(y_table),
        ],
        out_specs=[
            spec,
            spec,
            pl.BlockSpec((KY * 2 * Q, lanes), lambda x, c: (0, 0)),
            pl.BlockSpec((C * 8, 128), lambda x, c: (0, 0)),
        ],
        out_shape=[
            jax.ShapeDtypeStruct(cotangent.shape, BF16),
            jax.ShapeDtypeStruct(cotangent.shape, BF16),
            jax.ShapeDtypeStruct((KY * 2 * Q, lanes), F32),
            jax.ShapeDtypeStruct((C * 8, 128), F32),
        ],
        scratch_shapes=[
            pltpu.VMEM((KY * lanes, 2 * Q), F32),
            pltpu.VMEM((KY * lanes, 2 * Q), F32),
        ],
        compiler_params=pltpu.CompilerParams(vmem_limit_bytes=56 * MIB),
        cost_estimate=pl.CostEstimate(
            flops=5 * 10**9, bytes_accessed=42 * MIB, transcendentals=8 * 10**6
        ),
    )(back, early, cotangent, zt, zt_turned, y_back, y_table)


def last_kernel(back, early, zt_turned, y_back, out, gathered, *, lanes, block, group):
    plane, part = pl.program_id(0), pl.program_id(1)

    @pl.when((plane == 0) & (part == 0))
    def _():
        planes_layout(back, gathered, lanes)

    for g in range(0, block, group):
        own = y_inverse(gathered, y_back[...], plane * C + part * block + g, group, lanes)
        total = dot(own, zt_turned[...]).reshape(group, NY, CELLS)
        out[0, g : g + group] = (total + early[0, g : g + group].astype(F32)).astype(BF16)


def last(back, early, zt_turned, y_back, block=C, group=16):
    planes = early.shape[0]
    lanes = planes * C
    spec = pl.BlockSpec((1, block, NY, CELLS), lambda x, c: (x, c, 0, 0))
    return pl.pallas_call(
        functools.partial(last_kernel, lanes=lanes, block=block, group=group),
        grid=(planes, C // block),
        in_specs=[whole(back), spec, whole(zt_turned), whole(y_back)],
        out_specs=spec,
        out_shape=jax.ShapeDtypeStruct(early.shape, BF16),
        scratch_shapes=[pltpu.VMEM((KY * lanes, 2 * Q), F32)],
        compiler_params=pltpu.CompilerParams(vmem_limit_bytes=56 * MIB),
        cost_estimate=pl.CostEstimate(
            flops=2 * 10**9, bytes_accessed=17 * MIB, transcendentals=0
        ),
    )(back, early, zt_turned, y_back)


def on_device(hidden_field, cotangent, spectral_weight, local_weight, local_bias):
    planes, modes_here = hidden_field.shape[0], spectral_weight.shape[0]
    devices = lax.axis_size("gx")
    lanes = planes * C
    zt_host = zt_tables(modes_here)
    zt, zt_turned = jnp.asarray(zt_host), jnp.asarray(np.ascontiguousarray(zt_host.T))
    y_table, y_back = jnp.asarray(y_forward_table()), jnp.asarray(y_inverse_table())
    mask = jnp.asarray(diagonal_mask())
    tables = [jnp.asarray(table) for table in x_tables(planes, devices)] + [mask]

    pick, same = jnp.asarray(row_pick()), jnp.asarray(same_y())
    bias = jnp.repeat(local_bias, YB)[:, None]

    def exchange(value):
        return lax.all_to_all(value, "gx", split_axis=0, concat_axis=0, tiled=True)

    def to_owner(spectra):
        return exchange(spectra.reshape(devices, 2, modes_here, lanes))

    def to_slabs(back):
        return exchange(back).reshape(KY * 2 * Q, lanes)

    spectra = forward_planes(hidden_field, zt, y_table)
    early = local_term(hidden_field, local_weight.T, bias, pick, same)
    back, modes = mix_modes(to_owner(spectra), spectral_weight, tables)
    output, slope, dspectra, bias_part = middle(
        to_slabs(back), early, cotangent, zt, zt_turned, y_back, y_table
    )
    total = pointwise_gradient(hidden_field, slope, bias_part, pick, same)
    dback, dmodes = adjoint_modes(to_owner(dspectra), spectral_weight, tables)
    dback, slope, total = lax.optimization_barrier((dback, slope, total))
    late = late_term(slope, local_weight, pick, same)
    grad_spectral = mode_gradient(modes, dmodes, mask)
    span = 1
    while span < devices:
        total = total + lax.ppermute(total, "gx", [(d, d ^ span) for d in range(devices)])
        span *= 2
    grad_local = total[:8].reshape(8, 4, C).swapaxes(0, 1).reshape(C, C)
    grad_bias = total[8, :C]
    grad_field = last(to_slabs(dback), late, zt_turned, y_back)
    return (output, grad_field, grad_spectral, grad_local, grad_bias)


def solution(mesh):
    placed = (
        P(("groups", "gx"), None, None, None),
        P(("groups", "gx"), None, None, None),
        P("gx", None, None, None),
        P(),
        P(),
    )
    return jax.shard_map(
        on_device,
        mesh=mesh,
        in_specs=placed,
        out_specs=(
            P(("groups", "gx"), None, None, None),
            P(("groups", "gx"), None, None, None),
            P("gx", "groups", None, None),
            P("groups", None),
            P("groups"),
        ),
        check_vma=False,
    )
```

```python
import functools
import math

import jax
import jax.numpy as jnp
import ml_dtypes
import numpy as np
from jax import lax
from jax.experimental import pallas as pl
from jax.experimental.pallas import tpu as pltpu
from jax.sharding import PartitionSpec as P

NX, NY, NZ, NT = 128, 64, 64, 8
KX, KY, KZ, KT = 16, 16, 16, 4
C = 32
Q = KZ * KT
CELLS = NZ * NT
YB = 16
PIECE = 8
F32, BF16 = jnp.float32, jnp.bfloat16
HIGHEST = lax.Precision.HIGHEST
MIB = 1 << 20


def frequency(kept):
    serial = np.arange(kept)
    return np.where(serial < kept // 2, serial, serial - kept)


def angles(positions, length, kept):
    wound = (np.asarray(positions)[:, None] * frequency(kept)[None, :]) % length
    return 2.0 * math.pi / length * wound


def split2(table):
    high = table.astype(ml_dtypes.bfloat16)
    low = (table - high.astype(np.float64)).astype(ml_dtypes.bfloat16)
    return high, low


def stacked(table):
    high, low = split2(table)
    return np.concatenate([high, high, low], axis=1)


def zt_tables(modes_here):
    cells = np.arange(CELLS)
    depth, moment = cells // NT, cells % NT
    kept_z, kept_t = np.repeat(frequency(KZ), KT), np.tile(np.arange(KT), KZ)
    wound = (depth[:, None] * kept_z * NT + moment[:, None] * kept_t * NZ) % CELLS
    theta = 2.0 * math.pi / CELLS * wound
    cosine, sine = np.cos(theta), np.sin(theta)
    groups = Q // modes_here
    shape = (CELLS, groups, modes_here)
    cosine, sine = cosine.reshape(shape), sine.reshape(shape)
    first = np.stack([cosine, -sine], axis=2).reshape(CELLS, 2 * Q)
    second = np.stack([-sine, -cosine], axis=2).reshape(CELLS, 2 * Q)
    return np.concatenate([first, second], axis=1).astype(ml_dtypes.bfloat16)


def y_forward_table():
    theta = angles(np.arange(NY), NY, KY)
    table = np.concatenate([np.cos(theta), np.sin(theta)], axis=0).T
    high, low = split2(table)
    return np.concatenate([high, low], axis=0)


def y_inverse_table():
    theta = angles(np.arange(NY), NY, KY)
    table = np.concatenate([np.cos(theta), np.sin(theta)], axis=0)
    return stacked(table)


def x_tables(planes, devices):
    theta = angles(np.arange(devices) * planes, NX, KX).T
    cosine, sine = np.cos(theta), np.sin(theta)
    forward = np.block([[cosine, sine], [-sine, cosine]])
    turn = np.repeat(angles(np.arange(planes), NX, KX).T, C, axis=1)
    return (
        stacked(forward),
        stacked(forward.T),
        np.cos(turn).astype(np.float32),
        np.sin(turn).astype(np.float32),
    )


def diagonal_mask():
    return (np.arange(KX * C)[None, :] // C == np.arange(KX)[:, None]).astype(np.float32)


def halves(value):
    high = value.astype(BF16)
    return high, (value - high.astype(F32)).astype(BF16)


def three(value):
    high, low = halves(value)
    return jnp.concatenate([high, low, high], axis=0)


def dot(left, right):
    return jnp.dot(left, right, preferred_element_type=F32)


def lane_total(value, step):
    span = value.shape[1] // 2
    while span >= step:
        value = value + pltpu.roll(value, span, 1)
        span //= 2
    return value


def y_forward(sums, y_table, gathered, first_row, lanes):
    count = sums.shape[0] // NY
    for pair in range(0, count, 2):
        one = sums[pair * NY : (pair + 1) * NY].astype(BF16)
        two = sums[(pair + 1) * NY : (pair + 2) * NY].astype(BF16)
        right = jnp.concatenate(
            [
                jnp.concatenate([one[:, : 2 * Q], two[:, : 2 * Q]], axis=1),
                jnp.concatenate([one[:, 2 * Q :], two[:, 2 * Q :]], axis=1),
            ],
            axis=0,
        )
        both = dot(y_table, right)
        out = both[:KY] + both[KY:]
        gathered[pl.ds(first_row + pair, KY, stride=lanes), :] = out[:, : 2 * Q]
        gathered[pl.ds(first_row + pair + 1, KY, stride=lanes), :] = out[:, 2 * Q :]


def send_layout(gathered, out_ref, lanes):
    for ky in range(KY):
        out_ref[ky * 2 * Q : (ky + 1) * 2 * Q, :] = gathered[ky * lanes : (ky + 1) * lanes, :].T


def pieces(source, target, signals, plane, part):
    here = (plane, pl.ds(part * PIECE, PIECE))
    return pltpu.make_async_copy(
        source.at[here], target.at[here], signals.at[plane * (C // PIECE) + part]
    )


def each_piece(planes):
    return [(plane, part) for plane in range(planes) for part in range(C // PIECE)]


def in_hbm():
    return pl.BlockSpec(memory_space=pl.ANY)


def in_vmem():
    return pl.BlockSpec(memory_space=pltpu.VMEM)


def forward_kernel(field, zt, y_table, out, buffer, gathered, arrived, *, lanes, group):
    planes = field.shape[0]
    for plane, part in each_piece(planes):
        pieces(field, buffer, arrived, plane, part).start()

    def one_plane(plane, _):
        for c in range(0, C, group):
            for part in range(c // PIECE, (c + group) // PIECE):
                pieces(field, buffer, arrived, plane, part).wait()
            values = buffer[plane, c : c + group].reshape(group * NY, CELLS)
            y_forward(dot(values, zt[...]), y_table[...], gathered, plane * C + c, lanes)
        return 0

    lax.fori_loop(0, planes, one_plane, 0)
    send_layout(gathered, out, lanes)


def forward_planes(field, zt, y_table, group=C):
    planes = field.shape[0]
    lanes = planes * C
    return pl.pallas_call(
        functools.partial(forward_kernel, lanes=lanes, group=group),
        in_specs=[in_hbm(), in_vmem(), in_vmem()],
        out_specs=in_vmem(),
        out_shape=jax.ShapeDtypeStruct((KY * 2 * Q, lanes), F32),
        scratch_shapes=[
            pltpu.VMEM(field.shape, BF16),
            pltpu.VMEM((KY * lanes, 2 * Q), F32),
            pltpu.SemaphoreType.DMA((planes * (C // PIECE),)),
        ],
        compiler_params=pltpu.CompilerParams(vmem_limit_bytes=56 * MIB),
        cost_estimate=pl.CostEstimate(flops=2 * 10**9, bytes_accessed=9 * MIB, transcendentals=0),
    )(field, zt, y_table)


Q_BLOCK = 16


def modes_of(received, q_count, devices, lanes, forward, cosine, sine):
    columns = []
    for q in range(q_count):
        parts = [
            received[pl.ds(ri * q_count + q, devices, stride=2 * q_count), :] for ri in range(2)
        ]
        columns.append(jnp.concatenate(parts, axis=0))
    right = jnp.concatenate(columns, axis=1) if lanes % 128 == 0 else None
    found = []
    if right is not None:
        summed = dot(forward, three(right))
    for q in range(q_count):
        if right is not None:
            one = summed[:, q * lanes : (q + 1) * lanes]
        else:
            one = dot(forward, three(columns[q]))
        a_re, a_im = one[:KX], one[KX:]
        m_re = lane_total(a_re * cosine + a_im * sine, C)
        m_im = lane_total(a_im * cosine - a_re * sine, C)
        found.append((m_re, m_im))
    return found


def to_planes(mixed, out, q_count, devices, lanes, inverse, cosine, sine):
    turned = []
    for re, im in mixed:
        turned.append(
            jnp.concatenate([re * cosine - im * sine, re * sine + im * cosine], axis=0)
        )
    if lanes % 128 == 0:
        joined = jnp.concatenate(turned, axis=1)
        back = dot(inverse, three(joined))
        backs = [back[:, q * lanes : (q + 1) * lanes] for q in range(q_count)]
    else:
        backs = [dot(inverse, three(one)) for one in turned]
    for q in range(q_count):
        for ri in range(2):
            out[pl.ds(ri * q_count + q, devices, stride=2 * q_count), :] = backs[q][
                ri * devices : (ri + 1) * devices
            ]


def mode_factor(first, q):
    time_frequency = lax.rem(first + q, KT)
    return jnp.where(time_frequency == 0, 1.0, 2.0).astype(F32) / (NX * NY * NZ * NT)


def beside(one, two):
    if one.shape[1] < 128:
        return jnp.concatenate([one, two], axis=1)
    lane = lax.broadcasted_iota(jnp.int32, one.shape, 1)
    return jnp.where(lane < C, one, two)[:, : 2 * C]


def mix_kernel(
    received, weight, forward, inverse, cosine, sine, mask, out, modes_out, *, devices, lanes
):
    q_block = weight.shape[0]
    first = pl.program_id(0) * q_block
    flat_in = received.reshape(devices * 2 * q_block, lanes)
    flat_out = out.reshape(devices * 2 * q_block, lanes)
    modes = modes_of(flat_in, q_block, devices, lanes, forward[...], cosine[...], sine[...])
    own_block = jnp.concatenate([mask[...]] * 2, axis=0)
    mixed = []
    for q in range(q_block):
        re, im = modes[q]
        modes_out[q] = jnp.concatenate([re, im], axis=0)
        high, low = halves(jnp.concatenate([beside(re, -im), beside(im, re)], axis=0))
        product = dot(jnp.concatenate([high, low], axis=0), weight[q].reshape(2 * C, KX * C))
        kept = (product[: 2 * KX] + product[2 * KX :]) * own_block
        total = kept[:, :128]
        for column in range(128, KX * C, 128):
            total = total + kept[:, column : column + 128]
        total = lane_total(total, C)[:, :lanes] * mode_factor(first, q)
        pieces = (total[:KX], total[KX:])
        mixed.append(pieces)
    to_planes(mixed, flat_out, q_block, devices, lanes, inverse[...], cosine[...], sine[...])


def stage_kernel(*refs):
    count = len(refs) // 2
    sources, places, done = refs[:count], refs[count : 2 * count], refs[-1]
    copies = [
        pltpu.make_async_copy(source, place, done.at[i])
        for i, (source, place) in enumerate(zip(sources, places))
    ]
    for copy in copies:
        copy.start()
    for copy in copies:
        copy.wait()


def stage(*arrays):
    return pl.pallas_call(
        stage_kernel,
        in_specs=[pl.BlockSpec(memory_space=pl.ANY)] * len(arrays),
        out_specs=[in_vmem() for _ in arrays],
        out_shape=[pltpu.VMEM(array.shape, array.dtype) for array in arrays],
        scratch_shapes=[pltpu.SemaphoreType.DMA((len(arrays),))],
        cost_estimate=pl.CostEstimate(flops=0, bytes_accessed=6 * MIB, transcendentals=0),
    )(*arrays)


def whole(array):
    return pl.BlockSpec(array.shape, lambda *_: (0,) * array.ndim)


def mode_specs(devices, modes_here, lanes):
    q_block = min(Q_BLOCK, modes_here)
    slab = pl.BlockSpec((devices, 2, q_block, lanes), lambda s: (0, 0, s, 0))
    weight = pl.BlockSpec((q_block, 2, C, KX * C), lambda s: (s, 0, 0, 0))
    modes = pl.BlockSpec((q_block, 2 * KX, lanes), lambda s: (s, 0, 0))
    return slab, weight, modes


def mix_modes(received, weight, tables):
    devices, _, modes_here, lanes = received.shape
    slab, weight_spec, modes = mode_specs(devices, modes_here, lanes)
    return pl.pallas_call(
        functools.partial(mix_kernel, devices=devices, lanes=lanes),
        grid=(modes_here // min(Q_BLOCK, modes_here),),
        in_specs=[slab, weight_spec] + [whole(table) for table in tables],
        out_specs=[slab, modes],
        out_shape=[
            jax.ShapeDtypeStruct(received.shape, F32),
            jax.ShapeDtypeStruct((modes_here, 2 * KX, lanes), F32),
        ],
        compiler_params=pltpu.CompilerParams(vmem_limit_bytes=32 * MIB),
        cost_estimate=pl.CostEstimate(flops=10**9, bytes_accessed=5 * MIB, transcendentals=0),
    )(received, weight, *tables)


def spread(value, mask):
    if value.shape[1] < 128:
        value = jnp.concatenate([value] * (128 // value.shape[1]), axis=1)
    else:
        value = value[:, :128]
    return jnp.concatenate([value] * (KX * C // 128), axis=1) * mask


def adjoint_kernel(
    received, weight, forward, inverse, cosine, sine, mask, out, modes_out, *, devices, lanes
):
    q_block = weight.shape[0]
    first = pl.program_id(0) * q_block
    flat_in = received.reshape(devices * 2 * q_block, lanes)
    flat_out = out.reshape(devices * 2 * q_block, lanes)
    modes = modes_of(flat_in, q_block, devices, lanes, forward[...], cosine[...], sine[...])
    group = lax.broadcasted_iota(jnp.int32, (KX, 128), 1) // C
    odd = group % 2 == 1
    mixed = []
    for q in range(q_block):
        factor = mode_factor(first, q)
        d_re, d_im = modes[q][0] * factor, modes[q][1] * factor
        modes_out[q] = jnp.concatenate([d_re, d_im], axis=0)
        wide = jnp.concatenate([spread(d_re, mask[...]), spread(d_im, mask[...])], axis=0)
        high, low = halves(wide)
        left = jnp.concatenate([high, low], axis=0)
        right = jnp.concatenate([weight[q, 0], weight[q, 1]] * 2, axis=0)
        product = lax.dot_general(
            left, right, (((1,), (1,)), ((), ())), preferred_element_type=F32
        )
        product = product[: 2 * KX] + product[2 * KX :]
        re = product[:KX] + pltpu.roll(product[KX:], 128 - C, 1)
        im = product[KX:] - pltpu.roll(product[:KX], 128 - C, 1)
        re = jnp.where(odd, pltpu.roll(re, C, 1), re)
        im = jnp.where(odd, pltpu.roll(im, C, 1), im)
        mixed.append((re[:, :lanes], im[:, :lanes]))
    to_planes(mixed, flat_out, q_block, devices, lanes, inverse[...], cosine[...], sine[...])


def adjoint_modes(received, weight, tables):
    devices, _, modes_here, lanes = received.shape
    slab, weight_spec, modes = mode_specs(devices, modes_here, lanes)
    return pl.pallas_call(
        functools.partial(adjoint_kernel, devices=devices, lanes=lanes),
        grid=(modes_here // min(Q_BLOCK, modes_here),),
        in_specs=[slab, weight_spec] + [whole(table) for table in tables],
        out_specs=[slab, modes],
        out_shape=[
            jax.ShapeDtypeStruct(received.shape, F32),
            jax.ShapeDtypeStruct((modes_here, 2 * KX, lanes), F32),
        ],
        compiler_params=pltpu.CompilerParams(vmem_limit_bytes=32 * MIB),
        cost_estimate=pl.CostEstimate(flops=10**9, bytes_accessed=5 * MIB, transcendentals=0),
    )(received, weight, *tables)


def gradient_kernel(modes, dmodes, mask, out):
    for q in range(modes.shape[0]):
        left = modes[q][:, :C]
        l_high, l_low = halves(left)
        left = jnp.concatenate([l_high, l_high, l_low], axis=0)
        d_re, d_im = spread(dmodes[q, :KX], mask[...]), spread(dmodes[q, KX:], mask[...])
        for part, rows in ((0, (d_re, d_im)), (1, (d_im, -d_re))):
            high, low = halves(jnp.concatenate(rows, axis=0))
            right = jnp.concatenate([high, low, high], axis=0)
            out[q, part] = lax.dot_general(
                left, right, (((0,), (0,)), ((), ())), preferred_element_type=F32
            )


def mode_gradient(modes, dmodes, mask):
    modes_here, _, lanes = modes.shape
    q_block = min(Q_BLOCK, modes_here)
    spec = pl.BlockSpec((q_block, 2 * KX, lanes), lambda s: (s, 0, 0))
    return pl.pallas_call(
        gradient_kernel,
        grid=(modes_here // q_block,),
        in_specs=[spec, spec, whole(mask)],
        out_specs=pl.BlockSpec((q_block, 2, C, KX * C), lambda s: (s, 0, 0, 0)),
        out_shape=jax.ShapeDtypeStruct((modes_here, 2, C, KX * C), F32),
        compiler_params=pltpu.CompilerParams(vmem_limit_bytes=32 * MIB),
        cost_estimate=pl.CostEstimate(flops=10**8, bytes_accessed=5 * MIB, transcendentals=0),
    )(modes, dmodes, mask)


def planes_layout(back, gathered, lanes):
    for ky in range(KY):
        gathered[ky * lanes : (ky + 1) * lanes, :] = back[ky * 2 * Q : (ky + 1) * 2 * Q, :].T


def y_inverse(gathered, y_table, first_row, count, lanes):
    found = []
    for c in range(0, count, 2):
        row = first_row + c
        pair = jnp.concatenate(
            [
                gathered[pl.ds(row, KY, stride=lanes), :],
                gathered[pl.ds(row + 1, KY, stride=lanes), :],
            ],
            axis=1,
        )
        both = dot(y_table, three(pair)).astype(BF16)
        for k in range(2):
            columns = slice(k * 2 * Q, (k + 1) * 2 * Q)
            found.append(jnp.concatenate([both[:NY, columns], both[NY:, columns]], axis=1))
    return jnp.concatenate(found, axis=0)


def row_pick():
    return (np.arange(C * YB)[:, None] // YB == np.arange(C)[None, :]).astype(ml_dtypes.bfloat16)


def same_y():
    rows = np.arange(C * YB)
    return (rows[:, None] % YB == rows[None, :] % YB).astype(ml_dtypes.bfloat16)


def channel_map(weight, pick, same, out):
    rows = dot(pick, weight).astype(BF16)
    wide = lax.dot_general(rows, pick, (((1,), (1,)), ((), ())), preferred_element_type=F32)
    out[...] = wide.astype(BF16) * same


def local_kernel(field, weight, bias, pick, same, out, local):
    rows = C * YB

    @pl.when((pl.program_id(0) == 0) & (pl.program_id(1) == 0))
    def _():
        channel_map(weight[...], pick[...], same[...], local)

    for part in range(field.shape[2] // YB):
        y = slice(part * YB, (part + 1) * YB)
        total = dot(local[...], field[0, :, y].reshape(rows, CELLS)) + bias[...]
        out[0, :, y] = total.astype(BF16).reshape(C, YB, CELLS)


def local_term(field, weight, bias, pick, same, parts=1):
    block = pl.BlockSpec((1, C, NY // parts, CELLS), lambda x, y: (x, 0, y, 0))
    rows = C * YB
    return pl.pallas_call(
        local_kernel,
        grid=(field.shape[0], parts),
        in_specs=[block, whole(weight), whole(bias), whole(pick), whole(same)],
        out_specs=block,
        out_shape=jax.ShapeDtypeStruct(field.shape, BF16),
        scratch_shapes=[pltpu.VMEM((rows, rows), BF16)],
        compiler_params=pltpu.CompilerParams(vmem_limit_bytes=56 * MIB),
        cost_estimate=pl.CostEstimate(flops=4 * 10**9, bytes_accessed=17 * MIB, transcendentals=0),
    )(field, weight, bias, pick, same)


def late_kernel(slope, weight, pick, same, out, local):
    rows = C * YB

    @pl.when((pl.program_id(0) == 0) & (pl.program_id(1) == 0))
    def _():
        channel_map(weight[...], pick[...], same[...], local)

    for part in range(slope.shape[2] // YB):
        y = slice(part * YB, (part + 1) * YB)
        total = dot(local[...], slope[0, :, y].reshape(rows, CELLS))
        out[0, :, y] = total.astype(BF16).reshape(C, YB, CELLS)


def late_term(slope, weight, pick, same, parts=1):
    block = pl.BlockSpec((1, C, NY // parts, CELLS), lambda x, y: (x, 0, y, 0))
    rows = C * YB
    return pl.pallas_call(
        late_kernel,
        grid=(slope.shape[0], parts),
        in_specs=[block, whole(weight), whole(pick), whole(same)],
        out_specs=block,
        out_shape=jax.ShapeDtypeStruct(slope.shape, BF16),
        scratch_shapes=[pltpu.VMEM((rows, rows), BF16)],
        compiler_params=pltpu.CompilerParams(vmem_limit_bytes=56 * MIB),
        cost_estimate=pl.CostEstimate(flops=4 * 10**9, bytes_accessed=17 * MIB, transcendentals=0),
    )(slope, weight, pick, same)


def pointwise_kernel(field, slope, bias_part, pick, same, out, total):
    rows = C * YB
    first_step = (pl.program_id(0) == 0) & (pl.program_id(1) == 0)
    last_step = (pl.program_id(0) == pl.num_programs(0) - 1) & (
        pl.program_id(1) == pl.num_programs(1) - 1
    )

    @pl.when(first_step)
    def _():
        total[...] = jnp.zeros_like(total)

    for part in range(field.shape[2] // YB):
        y = slice(part * YB, (part + 1) * YB)
        total[...] += lax.dot_general(
            field[0, :, y].reshape(rows, CELLS),
            slope[0, :, y].reshape(rows, CELLS),
            (((1,), (1,)), ((), ())),
            preferred_element_type=F32,
        )

    @pl.when(last_step)
    def _():
        to_f32 = functools.partial(
            lax.dot_general, precision=HIGHEST, preferred_element_type=F32
        )
        chosen = pick[...].astype(F32)
        tiled = jnp.concatenate([chosen] * 4, axis=1)
        kept = total[...] * same[...].astype(F32)
        across = to_f32(kept, tiled, (((1,), (0,)), ((), ())))
        grads = to_f32(chosen, across, (((0,), (0,)), ((), ())))
        out[:C, :] = grads
        lane_sums = to_f32(jnp.ones((8, 128), F32), bias_part[...], (((1,), (1,)), ((), ())))
        by_channel = (
            lax.broadcasted_iota(jnp.int32, (8 * C, 128), 0) // 8
            == lax.broadcasted_iota(jnp.int32, (8 * C, 128), 1)
        ).astype(F32)
        out[C:, :] = to_f32(lane_sums, by_channel, (((1,), (0,)), ((), ())))


def pointwise_gradient(field, slope, bias_part, pick, same, parts=1):
    block = pl.BlockSpec((1, C, NY // parts, CELLS), lambda x, y: (x, 0, y, 0))
    rows = C * YB
    return pl.pallas_call(
        pointwise_kernel,
        grid=(field.shape[0], parts),
        in_specs=[block, block, whole(bias_part), whole(pick), whole(same)],
        out_specs=pl.BlockSpec((C + 8, 128), lambda x, y: (0, 0)),
        out_shape=jax.ShapeDtypeStruct((C + 8, 128), F32),
        scratch_shapes=[pltpu.VMEM((rows, rows), F32)],
        compiler_params=pltpu.CompilerParams(vmem_limit_bytes=56 * MIB),
        cost_estimate=pl.CostEstimate(flops=4 * 10**9, bytes_accessed=17 * MIB, transcendentals=0),
    )(field, slope, bias_part, pick, same)


def middle_kernel(
    back,
    early,
    cotangent,
    zt,
    zt_turned,
    y_back,
    y_table,
    out,
    slope_out,
    spectra,
    bias_grad,
    gathered,
    collected,
    *,
    lanes,
    block,
    group,
):
    plane, part = pl.program_id(0), pl.program_id(1)
    first_step = (plane == 0) & (part == 0)
    last_step = (plane == pl.num_programs(0) - 1) & (part == pl.num_programs(1) - 1)

    @pl.when(first_step)
    def _():
        planes_layout(back, gathered, lanes)
        bias_grad[...] = jnp.zeros_like(bias_grad)

    half_root = 1.0 / math.sqrt(2.0)
    for g in range(0, block, group):
        first_row = plane * C + part * block + g
        own = y_inverse(gathered, y_back[...], first_row, group, lanes)
        pre = dot(own, zt_turned[...])
        low = []
        for c in range(group):
            v = pre[c * NY : (c + 1) * NY] + early[0, g + c].astype(F32)
            grade = cotangent[0, g + c].astype(F32)
            normal = 0.5 + 0.5 * lax.erf(v * half_root)
            out[0, g + c] = (v * normal).astype(BF16)
            bell = jnp.exp(-0.5 * v * v) * (1.0 / math.sqrt(2.0 * math.pi))
            slope = grade * (normal + v * bell)
            low.append(slope.astype(BF16))
            slope_out[0, g + c] = low[-1]
            folded = slope[:, :128]
            for column in range(128, CELLS, 128):
                folded = folded + slope[:, column : column + 128]
            total = folded[:8]
            for row in range(8, NY, 8):
                total = total + folded[row : row + 8]
            r = pl.ds(pl.multiple_of((part * block + g + c) * 8, 8), 8)
            bias_grad[r, :] += total
        sums = dot(jnp.concatenate(low, axis=0), zt[...])
        y_forward(sums, y_table[...], collected, first_row, lanes)

    @pl.when(last_step)
    def _():
        send_layout(collected, spectra, lanes)


def middle(back, early, cotangent, zt, zt_turned, y_back, y_table, block=C, group=C):
    planes = cotangent.shape[0]
    lanes = planes * C
    spec = pl.BlockSpec((1, block, NY, CELLS), lambda x, c: (x, c, 0, 0))
    return pl.pallas_call(
        functools.partial(middle_kernel, lanes=lanes, block=block, group=group),
        grid=(planes, C // block),
        in_specs=[
            whole(back),
            spec,
            spec,
            in_vmem(),
            in_vmem(),
            in_vmem(),
            in_vmem(),
        ],
        out_specs=[
            spec,
            spec,
            pl.BlockSpec((KY * 2 * Q, lanes), lambda x, c: (0, 0)),
            pl.BlockSpec((C * 8, 128), lambda x, c: (0, 0)),
        ],
        out_shape=[
            jax.ShapeDtypeStruct(cotangent.shape, BF16),
            jax.ShapeDtypeStruct(cotangent.shape, BF16),
            jax.ShapeDtypeStruct((KY * 2 * Q, lanes), F32),
            jax.ShapeDtypeStruct((C * 8, 128), F32),
        ],
        scratch_shapes=[
            pltpu.VMEM((KY * lanes, 2 * Q), F32),
            pltpu.VMEM((KY * lanes, 2 * Q), F32),
        ],
        compiler_params=pltpu.CompilerParams(vmem_limit_bytes=50 * MIB),
        cost_estimate=pl.CostEstimate(
            flops=5 * 10**9, bytes_accessed=42 * MIB, transcendentals=8 * 10**6
        ),
    )(back, early, cotangent, zt, zt_turned, y_back, y_table)


def last_kernel(
    back,
    early,
    zt_turned,
    y_back,
    sums,
    out,
    local_grad,
    bias_grad,
    buffer,
    gathered,
    arrived,
    left,
    *,
    lanes,
    group,
):
    planes = early.shape[0]
    for plane, part in each_piece(planes):
        pieces(early, buffer, arrived, plane, part).start()
    planes_layout(back, gathered, lanes)
    local_grad[...] = sums[:C, :C]
    bias_grad[...] = sums[C : C + 1, :C]

    def one_plane(plane, _):
        for g in range(0, C, group):
            own = y_inverse(gathered, y_back[...], plane * C + g, group, lanes)
            total = dot(own, zt_turned[...]).reshape(group, NY, CELLS)
            parts = range(g // PIECE, (g + group) // PIECE)
            for part in parts:
                pieces(early, buffer, arrived, plane, part).wait()
            here = slice(g, g + group)
            buffer[plane, here] = (total + buffer[plane, here].astype(F32)).astype(BF16)
            for part in parts:
                pieces(buffer, out, left, plane, part).start()
        return 0

    lax.fori_loop(0, planes, one_plane, 0)
    for plane, part in each_piece(planes):
        pieces(buffer, out, left, plane, part).wait()


def last(back, early, zt_turned, y_back, sums, group=C):
    planes = early.shape[0]
    lanes = planes * C
    signals = pltpu.SemaphoreType.DMA((planes * (C // PIECE),))
    return pl.pallas_call(
        functools.partial(last_kernel, lanes=lanes, group=group),
        in_specs=[in_vmem(), in_hbm(), in_vmem(), in_vmem(), in_vmem()],
        out_specs=[in_hbm(), in_vmem(), in_vmem()],
        out_shape=[
            jax.ShapeDtypeStruct(early.shape, BF16),
            jax.ShapeDtypeStruct((C, C), F32),
            jax.ShapeDtypeStruct((1, C), F32),
        ],
        scratch_shapes=[
            pltpu.VMEM(early.shape, BF16),
            pltpu.VMEM((KY * lanes, 2 * Q), F32),
            signals,
            signals,
        ],
        compiler_params=pltpu.CompilerParams(vmem_limit_bytes=52 * MIB),
        cost_estimate=pl.CostEstimate(
            flops=2 * 10**9, bytes_accessed=17 * MIB, transcendentals=0
        ),
    )(back, early, zt_turned, y_back, sums)


def on_device(hidden_field, cotangent, spectral_weight, local_weight, local_bias):
    planes, modes_here = hidden_field.shape[0], spectral_weight.shape[0]
    devices = lax.axis_size("gx")
    lanes = planes * C
    zt_host = zt_tables(modes_here)
    zt, zt_turned = jnp.asarray(zt_host), jnp.asarray(np.ascontiguousarray(zt_host.T))
    y_table, y_back = jnp.asarray(y_forward_table()), jnp.asarray(y_inverse_table())
    mask = jnp.asarray(diagonal_mask())
    tables = [jnp.asarray(table) for table in x_tables(planes, devices)] + [mask]

    pick, same = jnp.asarray(row_pick()), jnp.asarray(same_y())
    bias = jnp.repeat(local_bias, YB)[:, None]

    def exchange(value):
        return lax.all_to_all(value, "gx", split_axis=0, concat_axis=0, tiled=True)

    def summed(value, span, end):
        while span < end:
            radix = 4 if 4 * span <= end else 2
            others = [
                lax.ppermute(value, "gx", [(d, d ^ (k * span)) for d in range(devices)])
                for k in range(1, radix)
            ]
            value = sum(others, value)
            span *= radix
        return value

    def to_owner(spectra):
        return exchange(spectra.reshape(devices, 2, modes_here, lanes))

    def to_slabs(back):
        return exchange(back).reshape(KY * 2 * Q, lanes)

    spectra = forward_planes(hidden_field, zt, y_table)
    zt, zt_turned, y_table, y_back = stage(zt, zt_turned, y_table, y_back)
    early = local_term(hidden_field, local_weight.T, bias, pick, same)
    back, modes = mix_modes(to_owner(spectra), spectral_weight, tables)
    output, slope, dspectra, bias_part = middle(
        to_slabs(back), early, cotangent, zt, zt_turned, y_back, y_table
    )
    total = pointwise_gradient(hidden_field, slope, bias_part, pick, same)
    dback, dmodes = adjoint_modes(to_owner(dspectra), spectral_weight, tables)
    near = min(devices, 8)
    total = summed(total, 1, near)
    dback, slope, total = lax.optimization_barrier((dback, slope, total))
    late = late_term(slope, local_weight, pick, same)
    grad_spectral = mode_gradient(modes, dmodes, mask)
    total = summed(total, near, devices)
    grad_field, grad_local, grad_bias = last(to_slabs(dback), late, zt_turned, y_back, total)
    grad_bias = grad_bias.reshape(C)
    return (output, grad_field, grad_spectral, grad_local, grad_bias)


def solution(mesh):
    placed = (
        P(("groups", "gx"), None, None, None),
        P(("groups", "gx"), None, None, None),
        P("gx", None, None, None),
        P(),
        P(),
    )
    return jax.shard_map(
        on_device,
        mesh=mesh,
        in_specs=placed,
        out_specs=(
            P(("groups", "gx"), None, None, None),
            P(("groups", "gx"), None, None, None),
            P("gx", "groups", None, None),
            P("groups", None),
            P("groups"),
        ),
        check_vma=False,
    )
```

```python
import functools
import math

import jax
import jax.numpy as jnp
import ml_dtypes
import numpy as np
from jax import lax
from jax.experimental import pallas as pl
from jax.experimental.pallas import tpu as pltpu
from jax.sharding import PartitionSpec as P

NX, NY, NZ, NT = 128, 64, 64, 8
KX, KY, KZ, KT = 16, 16, 16, 4
C = 32
Q = KZ * KT
CELLS = NZ * NT
YB = 16
PIECE = 16
AHEAD = 4
F32, BF16 = jnp.float32, jnp.bfloat16
HIGHEST = lax.Precision.HIGHEST
MIB = 1 << 20


def frequency(kept):
    serial = np.arange(kept)
    return np.where(serial < kept // 2, serial, serial - kept)


def angles(positions, length, kept):
    wound = (np.asarray(positions)[:, None] * frequency(kept)[None, :]) % length
    return 2.0 * math.pi / length * wound


def split2(table):
    high = table.astype(ml_dtypes.bfloat16)
    low = (table - high.astype(np.float64)).astype(ml_dtypes.bfloat16)
    return high, low


def stacked(table):
    high, low = split2(table)
    return np.concatenate([high, high, low], axis=1)


def zt_tables(modes_here):
    cells = np.arange(CELLS)
    depth, moment = cells // NT, cells % NT
    kept_z, kept_t = np.repeat(frequency(KZ), KT), np.tile(np.arange(KT), KZ)
    wound = (depth[:, None] * kept_z * NT + moment[:, None] * kept_t * NZ) % CELLS
    theta = 2.0 * math.pi / CELLS * wound
    cosine, sine = np.cos(theta), np.sin(theta)
    groups = Q // modes_here
    shape = (CELLS, groups, modes_here)
    cosine, sine = cosine.reshape(shape), sine.reshape(shape)
    first = np.stack([cosine, -sine], axis=2).reshape(CELLS, 2 * Q)
    second = np.stack([-sine, -cosine], axis=2).reshape(CELLS, 2 * Q)
    return np.concatenate([first, second], axis=1).astype(ml_dtypes.bfloat16)


def y_forward_table():
    theta = angles(np.arange(NY), NY, KY)
    table = np.concatenate([np.cos(theta), np.sin(theta)], axis=0).T
    high, low = split2(table)
    return np.concatenate([high, low], axis=0)


def y_inverse_table():
    theta = angles(np.arange(NY), NY, KY)
    table = np.concatenate([np.cos(theta), np.sin(theta)], axis=0)
    return stacked(table)


def x_tables(planes, devices):
    theta = angles(np.arange(devices) * planes, NX, KX).T
    cosine, sine = np.cos(theta), np.sin(theta)
    forward = np.block([[cosine, sine], [-sine, cosine]])
    turn = np.repeat(angles(np.arange(planes), NX, KX).T, C, axis=1)
    return (
        stacked(forward),
        stacked(forward.T),
        np.cos(turn).astype(np.float32),
        np.sin(turn).astype(np.float32),
    )


def diagonal_mask():
    return (np.arange(KX * C)[None, :] // C == np.arange(KX)[:, None]).astype(np.float32)


def halves(value):
    high = value.astype(BF16)
    return high, (value - high.astype(F32)).astype(BF16)


def three(value):
    high, low = halves(value)
    return jnp.concatenate([high, low, high], axis=0)


def dot(left, right):
    return jnp.dot(left, right, preferred_element_type=F32)


def lane_total(value, step):
    span = value.shape[1] // 2
    while span >= step:
        value = value + pltpu.roll(value, span, 1)
        span //= 2
    return value


def y_forward(sums, y_table, gathered, first_row, lanes):
    count = sums.shape[0] // NY
    for pair in range(0, count, 2):
        one = sums[pair * NY : (pair + 1) * NY].astype(BF16)
        two = sums[(pair + 1) * NY : (pair + 2) * NY].astype(BF16)
        right = jnp.concatenate(
            [
                jnp.concatenate([one[:, : 2 * Q], two[:, : 2 * Q]], axis=1),
                jnp.concatenate([one[:, 2 * Q :], two[:, 2 * Q :]], axis=1),
            ],
            axis=0,
        )
        both = dot(y_table, right)
        out = both[:KY] + both[KY:]
        gathered[pl.ds(first_row + pair, KY, stride=lanes), :] = out[:, : 2 * Q]
        gathered[pl.ds(first_row + pair + 1, KY, stride=lanes), :] = out[:, 2 * Q :]


def send_layout(gathered, out_ref, lanes):
    for ky in range(KY):
        out_ref[ky * 2 * Q : (ky + 1) * 2 * Q, :] = gathered[ky * lanes : (ky + 1) * lanes, :].T


def pieces(source, target, signals, plane, part):
    here = (plane, pl.ds(part * PIECE, PIECE))
    return pltpu.make_async_copy(
        source.at[here], target.at[here], signals.at[plane * (C // PIECE) + part]
    )


def plane_copies(source, target, signals, plane):
    return [pieces(source, target, signals, plane, part) for part in range(C // PIECE)]


def start_plane(source, target, signals, plane):
    for copy in plane_copies(source, target, signals, plane):
        copy.start()


def wait_plane(source, target, signals, plane):
    for copy in plane_copies(source, target, signals, plane):
        copy.wait()


def in_hbm():
    return pl.BlockSpec(memory_space=pl.ANY)


def in_vmem():
    return pl.BlockSpec(memory_space=pltpu.VMEM)


def forward_kernel(field, zt, y_table, out, buffer, gathered, arrived, *, lanes, group):
    planes = field.shape[0]
    for plane in range(min(AHEAD, planes)):
        start_plane(field, buffer, arrived, plane)

    def one_plane(plane, _):
        wait_plane(field, buffer, arrived, plane)

        @pl.when(plane + AHEAD < planes)
        def _():
            start_plane(field, buffer, arrived, plane + AHEAD)

        for c in range(0, C, group):
            values = buffer[plane, c : c + group].reshape(group * NY, CELLS)
            y_forward(dot(values, zt[...]), y_table[...], gathered, plane * C + c, lanes)
        return 0

    lax.fori_loop(0, planes, one_plane, 0)
    send_layout(gathered, out, lanes)


def forward_planes(field, zt, y_table, group=C):
    planes = field.shape[0]
    lanes = planes * C
    return pl.pallas_call(
        functools.partial(forward_kernel, lanes=lanes, group=group),
        in_specs=[in_hbm(), in_vmem(), in_vmem()],
        out_specs=in_vmem(),
        out_shape=jax.ShapeDtypeStruct((KY * 2 * Q, lanes), F32),
        scratch_shapes=[
            pltpu.VMEM(field.shape, BF16),
            pltpu.VMEM((KY * lanes, 2 * Q), F32),
            pltpu.SemaphoreType.DMA((planes * (C // PIECE),)),
        ],
        compiler_params=pltpu.CompilerParams(vmem_limit_bytes=56 * MIB),
        cost_estimate=pl.CostEstimate(flops=2 * 10**9, bytes_accessed=9 * MIB, transcendentals=0),
    )(field, zt, y_table)


Q_BLOCK = 16


def modes_of(received, q_count, devices, lanes, forward, cosine, sine):
    columns = []
    for q in range(q_count):
        parts = [
            received[pl.ds(ri * q_count + q, devices, stride=2 * q_count), :] for ri in range(2)
        ]
        columns.append(jnp.concatenate(parts, axis=0))
    right = jnp.concatenate(columns, axis=1) if lanes % 128 == 0 else None
    found = []
    if right is not None:
        summed = dot(forward, three(right))
    for q in range(q_count):
        if right is not None:
            one = summed[:, q * lanes : (q + 1) * lanes]
        else:
            one = dot(forward, three(columns[q]))
        a_re, a_im = one[:KX], one[KX:]
        m_re = lane_total(a_re * cosine + a_im * sine, C)
        m_im = lane_total(a_im * cosine - a_re * sine, C)
        found.append((m_re, m_im))
    return found


def to_planes(mixed, out, q_count, devices, lanes, inverse, cosine, sine):
    turned = []
    for re, im in mixed:
        turned.append(
            jnp.concatenate([re * cosine - im * sine, re * sine + im * cosine], axis=0)
        )
    if lanes % 128 == 0:
        joined = jnp.concatenate(turned, axis=1)
        back = dot(inverse, three(joined))
        backs = [back[:, q * lanes : (q + 1) * lanes] for q in range(q_count)]
    else:
        backs = [dot(inverse, three(one)) for one in turned]
    for q in range(q_count):
        for ri in range(2):
            out[pl.ds(ri * q_count + q, devices, stride=2 * q_count), :] = backs[q][
                ri * devices : (ri + 1) * devices
            ]


def mode_factor(first, q):
    time_frequency = lax.rem(first + q, KT)
    return jnp.where(time_frequency == 0, 1.0, 2.0).astype(F32) / (NX * NY * NZ * NT)


def beside(one, two):
    if one.shape[1] < 128:
        return jnp.concatenate([one, two], axis=1)
    lane = lax.broadcasted_iota(jnp.int32, one.shape, 1)
    return jnp.where(lane < C, one, two)[:, : 2 * C]


def mix_kernel(
    received, weight, forward, inverse, cosine, sine, mask, out, modes_out, *, devices, lanes
):
    q_block = weight.shape[0]
    first = pl.program_id(0) * q_block
    flat_in = received.reshape(devices * 2 * q_block, lanes)
    flat_out = out.reshape(devices * 2 * q_block, lanes)
    modes = modes_of(flat_in, q_block, devices, lanes, forward[...], cosine[...], sine[...])
    own_block = jnp.concatenate([mask[...]] * 2, axis=0)
    mixed = []
    for q in range(q_block):
        re, im = modes[q]
        modes_out[q] = jnp.concatenate([re, im], axis=0)
        high, low = halves(jnp.concatenate([beside(re, -im), beside(im, re)], axis=0))
        product = dot(jnp.concatenate([high, low], axis=0), weight[q].reshape(2 * C, KX * C))
        kept = (product[: 2 * KX] + product[2 * KX :]) * own_block
        total = kept[:, :128]
        for column in range(128, KX * C, 128):
            total = total + kept[:, column : column + 128]
        total = lane_total(total, C)[:, :lanes] * mode_factor(first, q)
        pieces = (total[:KX], total[KX:])
        mixed.append(pieces)
    to_planes(mixed, flat_out, q_block, devices, lanes, inverse[...], cosine[...], sine[...])


def stage_kernel(*refs):
    count = len(refs) // 2
    sources, places, done = refs[:count], refs[count : 2 * count], refs[-1]
    copies = [
        pltpu.make_async_copy(source, place, done.at[i])
        for i, (source, place) in enumerate(zip(sources, places))
    ]
    for copy in copies:
        copy.start()
    for copy in copies:
        copy.wait()


def stage(*arrays):
    return pl.pallas_call(
        stage_kernel,
        in_specs=[pl.BlockSpec(memory_space=pl.ANY)] * len(arrays),
        out_specs=[in_vmem() for _ in arrays],
        out_shape=[pltpu.VMEM(array.shape, array.dtype) for array in arrays],
        scratch_shapes=[pltpu.SemaphoreType.DMA((len(arrays),))],
        cost_estimate=pl.CostEstimate(flops=0, bytes_accessed=6 * MIB, transcendentals=0),
    )(*arrays)


def whole(array):
    return pl.BlockSpec(array.shape, lambda *_: (0,) * array.ndim)


def mode_specs(devices, modes_here, lanes):
    q_block = min(Q_BLOCK, modes_here)
    slab = pl.BlockSpec((devices, 2, q_block, lanes), lambda s: (0, 0, s, 0))
    weight = pl.BlockSpec((q_block, 2, C, KX * C), lambda s: (s, 0, 0, 0))
    modes = pl.BlockSpec((q_block, 2 * KX, lanes), lambda s: (s, 0, 0))
    return slab, weight, modes


def mix_modes(received, weight, tables):
    devices, _, modes_here, lanes = received.shape
    slab, weight_spec, modes = mode_specs(devices, modes_here, lanes)
    return pl.pallas_call(
        functools.partial(mix_kernel, devices=devices, lanes=lanes),
        grid=(modes_here // min(Q_BLOCK, modes_here),),
        in_specs=[slab, weight_spec] + [whole(table) for table in tables],
        out_specs=[slab, modes],
        out_shape=[
            jax.ShapeDtypeStruct(received.shape, F32),
            jax.ShapeDtypeStruct((modes_here, 2 * KX, lanes), F32),
        ],
        compiler_params=pltpu.CompilerParams(vmem_limit_bytes=32 * MIB),
        cost_estimate=pl.CostEstimate(flops=10**9, bytes_accessed=5 * MIB, transcendentals=0),
    )(received, weight, *tables)


def spread(value, mask):
    if value.shape[1] < 128:
        value = jnp.concatenate([value] * (128 // value.shape[1]), axis=1)
    else:
        value = value[:, :128]
    return jnp.concatenate([value] * (KX * C // 128), axis=1) * mask


def adjoint_kernel(
    received, weight, forward, inverse, cosine, sine, mask, out, modes_out, *, devices, lanes
):
    q_block = weight.shape[0]
    first = pl.program_id(0) * q_block
    flat_in = received.reshape(devices * 2 * q_block, lanes)
    flat_out = out.reshape(devices * 2 * q_block, lanes)
    modes = modes_of(flat_in, q_block, devices, lanes, forward[...], cosine[...], sine[...])
    group = lax.broadcasted_iota(jnp.int32, (KX, 128), 1) // C
    odd = group % 2 == 1
    mixed = []
    for q in range(q_block):
        factor = mode_factor(first, q)
        d_re, d_im = modes[q][0] * factor, modes[q][1] * factor
        modes_out[q] = jnp.concatenate([d_re, d_im], axis=0)
        wide = jnp.concatenate([spread(d_re, mask[...]), spread(d_im, mask[...])], axis=0)
        high, low = halves(wide)
        left = jnp.concatenate([high, low], axis=0)
        right = jnp.concatenate([weight[q, 0], weight[q, 1]] * 2, axis=0)
        product = lax.dot_general(
            left, right, (((1,), (1,)), ((), ())), preferred_element_type=F32
        )
        product = product[: 2 * KX] + product[2 * KX :]
        re = product[:KX] + pltpu.roll(product[KX:], 128 - C, 1)
        im = product[KX:] - pltpu.roll(product[:KX], 128 - C, 1)
        re = jnp.where(odd, pltpu.roll(re, C, 1), re)
        im = jnp.where(odd, pltpu.roll(im, C, 1), im)
        mixed.append((re[:, :lanes], im[:, :lanes]))
    to_planes(mixed, flat_out, q_block, devices, lanes, inverse[...], cosine[...], sine[...])


def adjoint_modes(received, weight, tables):
    devices, _, modes_here, lanes = received.shape
    slab, weight_spec, modes = mode_specs(devices, modes_here, lanes)
    return pl.pallas_call(
        functools.partial(adjoint_kernel, devices=devices, lanes=lanes),
        grid=(modes_here // min(Q_BLOCK, modes_here),),
        in_specs=[slab, weight_spec] + [whole(table) for table in tables],
        out_specs=[slab, modes],
        out_shape=[
            jax.ShapeDtypeStruct(received.shape, F32),
            jax.ShapeDtypeStruct((modes_here, 2 * KX, lanes), F32),
        ],
        compiler_params=pltpu.CompilerParams(vmem_limit_bytes=32 * MIB),
        cost_estimate=pl.CostEstimate(flops=10**9, bytes_accessed=5 * MIB, transcendentals=0),
    )(received, weight, *tables)


def gradient_kernel(modes, dmodes, mask, out):
    for q in range(modes.shape[0]):
        left = modes[q][:, :C]
        l_high, l_low = halves(left)
        left = jnp.concatenate([l_high, l_high, l_low], axis=0)
        d_re, d_im = spread(dmodes[q, :KX], mask[...]), spread(dmodes[q, KX:], mask[...])
        for part, rows in ((0, (d_re, d_im)), (1, (d_im, -d_re))):
            high, low = halves(jnp.concatenate(rows, axis=0))
            right = jnp.concatenate([high, low, high], axis=0)
            out[q, part] = lax.dot_general(
                left, right, (((0,), (0,)), ((), ())), preferred_element_type=F32
            )


def mode_gradient(modes, dmodes, mask):
    modes_here, _, lanes = modes.shape
    q_block = min(Q_BLOCK, modes_here)
    spec = pl.BlockSpec((q_block, 2 * KX, lanes), lambda s: (s, 0, 0))
    return pl.pallas_call(
        gradient_kernel,
        grid=(modes_here // q_block,),
        in_specs=[spec, spec, whole(mask)],
        out_specs=pl.BlockSpec((q_block, 2, C, KX * C), lambda s: (s, 0, 0, 0)),
        out_shape=jax.ShapeDtypeStruct((modes_here, 2, C, KX * C), F32),
        compiler_params=pltpu.CompilerParams(vmem_limit_bytes=32 * MIB),
        cost_estimate=pl.CostEstimate(flops=10**8, bytes_accessed=5 * MIB, transcendentals=0),
    )(modes, dmodes, mask)


def planes_layout(back, gathered, lanes):
    for ky in range(KY):
        gathered[ky * lanes : (ky + 1) * lanes, :] = back[ky * 2 * Q : (ky + 1) * 2 * Q, :].T


def y_inverse(gathered, y_table, first_row, count, lanes):
    found = []
    for c in range(0, count, 2):
        row = first_row + c
        pair = jnp.concatenate(
            [
                gathered[pl.ds(row, KY, stride=lanes), :],
                gathered[pl.ds(row + 1, KY, stride=lanes), :],
            ],
            axis=1,
        )
        both = dot(y_table, three(pair)).astype(BF16)
        for k in range(2):
            columns = slice(k * 2 * Q, (k + 1) * 2 * Q)
            found.append(jnp.concatenate([both[:NY, columns], both[NY:, columns]], axis=1))
    return jnp.concatenate(found, axis=0)


def row_pick():
    return (np.arange(C * YB)[:, None] // YB == np.arange(C)[None, :]).astype(ml_dtypes.bfloat16)


def same_y():
    rows = np.arange(C * YB)
    return (rows[:, None] % YB == rows[None, :] % YB).astype(ml_dtypes.bfloat16)


def channel_map(weight, pick, same, out):
    rows = dot(pick, weight).astype(BF16)
    wide = lax.dot_general(rows, pick, (((1,), (1,)), ((), ())), preferred_element_type=F32)
    out[...] = wide.astype(BF16) * same


def local_kernel(field, weight, bias, pick, same, out, local):
    rows = C * YB

    @pl.when((pl.program_id(0) == 0) & (pl.program_id(1) == 0))
    def _():
        channel_map(weight[...], pick[...], same[...], local)

    for part in range(field.shape[2] // YB):
        y = slice(part * YB, (part + 1) * YB)
        total = dot(local[...], field[0, :, y].reshape(rows, CELLS)) + bias[...]
        out[0, :, y] = total.astype(BF16).reshape(C, YB, CELLS)


def local_term(field, weight, bias, pick, same, parts=1):
    block = pl.BlockSpec((1, C, NY // parts, CELLS), lambda x, y: (x, 0, y, 0))
    rows = C * YB
    return pl.pallas_call(
        local_kernel,
        grid=(field.shape[0], parts),
        in_specs=[block, whole(weight), whole(bias), whole(pick), whole(same)],
        out_specs=block,
        out_shape=jax.ShapeDtypeStruct(field.shape, BF16),
        scratch_shapes=[pltpu.VMEM((rows, rows), BF16)],
        compiler_params=pltpu.CompilerParams(vmem_limit_bytes=56 * MIB),
        cost_estimate=pl.CostEstimate(flops=4 * 10**9, bytes_accessed=17 * MIB, transcendentals=0),
    )(field, weight, bias, pick, same)


def late_kernel(slope, weight, pick, same, out, local):
    rows = C * YB

    @pl.when((pl.program_id(0) == 0) & (pl.program_id(1) == 0))
    def _():
        channel_map(weight[...], pick[...], same[...], local)

    for part in range(slope.shape[2] // YB):
        y = slice(part * YB, (part + 1) * YB)
        total = dot(local[...], slope[0, :, y].reshape(rows, CELLS))
        out[0, :, y] = total.astype(BF16).reshape(C, YB, CELLS)


def late_term(slope, weight, pick, same, parts=1):
    block = pl.BlockSpec((1, C, NY // parts, CELLS), lambda x, y: (x, 0, y, 0))
    rows = C * YB
    return pl.pallas_call(
        late_kernel,
        grid=(slope.shape[0], parts),
        in_specs=[block, whole(weight), whole(pick), whole(same)],
        out_specs=block,
        out_shape=jax.ShapeDtypeStruct(slope.shape, BF16),
        scratch_shapes=[pltpu.VMEM((rows, rows), BF16)],
        compiler_params=pltpu.CompilerParams(vmem_limit_bytes=56 * MIB),
        cost_estimate=pl.CostEstimate(flops=4 * 10**9, bytes_accessed=17 * MIB, transcendentals=0),
    )(slope, weight, pick, same)


def pointwise_kernel(field, slope, bias_part, pick, same, out, total):
    rows = C * YB
    first_step = (pl.program_id(0) == 0) & (pl.program_id(1) == 0)
    last_step = (pl.program_id(0) == pl.num_programs(0) - 1) & (
        pl.program_id(1) == pl.num_programs(1) - 1
    )

    @pl.when(first_step)
    def _():
        total[...] = jnp.zeros_like(total)

    for part in range(field.shape[2] // YB):
        y = slice(part * YB, (part + 1) * YB)
        total[...] += lax.dot_general(
            field[0, :, y].reshape(rows, CELLS),
            slope[0, :, y].reshape(rows, CELLS),
            (((1,), (1,)), ((), ())),
            preferred_element_type=F32,
        )

    @pl.when(last_step)
    def _():
        to_f32 = functools.partial(
            lax.dot_general, precision=HIGHEST, preferred_element_type=F32
        )
        chosen = pick[...].astype(F32)
        tiled = jnp.concatenate([chosen] * 4, axis=1)
        kept = total[...] * same[...].astype(F32)
        across = to_f32(kept, tiled, (((1,), (0,)), ((), ())))
        grads = to_f32(chosen, across, (((0,), (0,)), ((), ())))
        out[:C, :] = grads
        lane_sums = to_f32(jnp.ones((8, 128), F32), bias_part[...], (((1,), (1,)), ((), ())))
        by_channel = (
            lax.broadcasted_iota(jnp.int32, (8 * C, 128), 0) // 8
            == lax.broadcasted_iota(jnp.int32, (8 * C, 128), 1)
        ).astype(F32)
        out[C:, :] = to_f32(lane_sums, by_channel, (((1,), (0,)), ((), ())))


def pointwise_gradient(field, slope, bias_part, pick, same, parts=1):
    block = pl.BlockSpec((1, C, NY // parts, CELLS), lambda x, y: (x, 0, y, 0))
    rows = C * YB
    return pl.pallas_call(
        pointwise_kernel,
        grid=(field.shape[0], parts),
        in_specs=[block, block, whole(bias_part), whole(pick), whole(same)],
        out_specs=pl.BlockSpec((C + 8, 128), lambda x, y: (0, 0)),
        out_shape=jax.ShapeDtypeStruct((C + 8, 128), F32),
        scratch_shapes=[pltpu.VMEM((rows, rows), F32)],
        compiler_params=pltpu.CompilerParams(vmem_limit_bytes=56 * MIB),
        cost_estimate=pl.CostEstimate(flops=4 * 10**9, bytes_accessed=17 * MIB, transcendentals=0),
    )(field, slope, bias_part, pick, same)


def middle_kernel(
    back,
    early,
    cotangent,
    zt,
    zt_turned,
    y_back,
    y_table,
    out,
    slope_out,
    spectra,
    bias_grad,
    left,
    right,
    gathered,
    collected,
    left_in,
    right_in,
    left_out,
    right_out,
    *,
    lanes,
    group,
):
    planes = cotangent.shape[0]
    for plane in range(min(AHEAD, planes)):
        start_plane(early, left, left_in, plane)
        start_plane(cotangent, right, right_in, plane)
    planes_layout(back, gathered, lanes)
    bias_grad[...] = jnp.zeros_like(bias_grad)
    half_root = 1.0 / math.sqrt(2.0)

    def one_plane(plane, _):
        wait_plane(early, left, left_in, plane)
        wait_plane(cotangent, right, right_in, plane)

        @pl.when(plane + AHEAD < planes)
        def _():
            start_plane(early, left, left_in, plane + AHEAD)
            start_plane(cotangent, right, right_in, plane + AHEAD)

        for g in range(0, C, group):
            own = y_inverse(gathered, y_back[...], plane * C + g, group, lanes)
            pre = dot(own, zt_turned[...])
            parts = range(g // PIECE, (g + group) // PIECE)
            low = []
            for c in range(group):
                v = pre[c * NY : (c + 1) * NY] + left[plane, g + c].astype(F32)
                grade = right[plane, g + c].astype(F32)
                normal = 0.5 + 0.5 * lax.erf(v * half_root)
                left[plane, g + c] = (v * normal).astype(BF16)
                bell = jnp.exp(-0.5 * v * v) * (1.0 / math.sqrt(2.0 * math.pi))
                slope = grade * (normal + v * bell)
                low.append(slope.astype(BF16))
                right[plane, g + c] = low[-1]
                folded = slope[:, :128]
                for column in range(128, CELLS, 128):
                    folded = folded + slope[:, column : column + 128]
                total = folded[:8]
                for row in range(8, NY, 8):
                    total = total + folded[row : row + 8]
                bias_grad[(g + c) * 8 : (g + c + 1) * 8, :] += total
            for part in parts:
                pieces(left, out, left_out, plane, part).start()
                pieces(right, slope_out, right_out, plane, part).start()
            sums = dot(jnp.concatenate(low, axis=0), zt[...])
            y_forward(sums, y_table[...], collected, plane * C + g, lanes)
        return 0

    lax.fori_loop(0, planes, one_plane, 0)
    send_layout(collected, spectra, lanes)
    for plane in range(planes):
        wait_plane(left, out, left_out, plane)
        wait_plane(right, slope_out, right_out, plane)


def middle(back, early, cotangent, zt, zt_turned, y_back, y_table, group=C):
    planes = cotangent.shape[0]
    lanes = planes * C
    signals = pltpu.SemaphoreType.DMA((planes * (C // PIECE),))
    return pl.pallas_call(
        functools.partial(middle_kernel, lanes=lanes, group=group),
        in_specs=[in_vmem(), in_hbm(), in_hbm()] + [in_vmem()] * 4,
        out_specs=[in_hbm(), in_hbm(), in_vmem(), in_vmem()],
        out_shape=[
            jax.ShapeDtypeStruct(cotangent.shape, BF16),
            jax.ShapeDtypeStruct(cotangent.shape, BF16),
            jax.ShapeDtypeStruct((KY * 2 * Q, lanes), F32),
            jax.ShapeDtypeStruct((C * 8, 128), F32),
        ],
        scratch_shapes=[
            pltpu.VMEM(cotangent.shape, BF16),
            pltpu.VMEM(cotangent.shape, BF16),
            pltpu.VMEM((KY * lanes, 2 * Q), F32),
            pltpu.VMEM((KY * lanes, 2 * Q), F32),
            signals,
            signals,
            signals,
            signals,
        ],
        compiler_params=pltpu.CompilerParams(vmem_limit_bytes=48 * MIB),
        cost_estimate=pl.CostEstimate(
            flops=5 * 10**9, bytes_accessed=34 * MIB, transcendentals=8 * 10**6
        ),
    )(back, early, cotangent, zt, zt_turned, y_back, y_table)


def last_kernel(
    back,
    early,
    zt_turned,
    y_back,
    sums,
    out,
    local_grad,
    bias_grad,
    buffer,
    gathered,
    arrived,
    left,
    *,
    lanes,
    group,
):
    planes = early.shape[0]
    for plane in range(min(AHEAD, planes)):
        start_plane(early, buffer, arrived, plane)
    planes_layout(back, gathered, lanes)
    local_grad[...] = sums[:C, :C]
    bias_grad[...] = sums[C : C + 1, :C]

    def one_plane(plane, _):
        wait_plane(early, buffer, arrived, plane)

        @pl.when(plane + AHEAD < planes)
        def _():
            start_plane(early, buffer, arrived, plane + AHEAD)

        for g in range(0, C, group):
            own = y_inverse(gathered, y_back[...], plane * C + g, group, lanes)
            total = dot(own, zt_turned[...]).reshape(group, NY, CELLS)
            here = slice(g, g + group)
            buffer[plane, here] = (total + buffer[plane, here].astype(F32)).astype(BF16)
            for part in range(g // PIECE, (g + group) // PIECE):
                pieces(buffer, out, left, plane, part).start()
        return 0

    lax.fori_loop(0, planes, one_plane, 0)
    for plane in range(planes):
        wait_plane(buffer, out, left, plane)


def last(back, early, zt_turned, y_back, sums, group=C):
    planes = early.shape[0]
    lanes = planes * C
    signals = pltpu.SemaphoreType.DMA((planes * (C // PIECE),))
    return pl.pallas_call(
        functools.partial(last_kernel, lanes=lanes, group=group),
        in_specs=[in_vmem(), in_hbm(), in_vmem(), in_vmem(), in_vmem()],
        out_specs=[in_hbm(), in_vmem(), in_vmem()],
        out_shape=[
            jax.ShapeDtypeStruct(early.shape, BF16),
            jax.ShapeDtypeStruct((C, C), F32),
            jax.ShapeDtypeStruct((1, C), F32),
        ],
        scratch_shapes=[
            pltpu.VMEM(early.shape, BF16),
            pltpu.VMEM((KY * lanes, 2 * Q), F32),
            signals,
            signals,
        ],
        compiler_params=pltpu.CompilerParams(vmem_limit_bytes=52 * MIB),
        cost_estimate=pl.CostEstimate(
            flops=2 * 10**9, bytes_accessed=17 * MIB, transcendentals=0
        ),
    )(back, early, zt_turned, y_back, sums)


def on_device(hidden_field, cotangent, spectral_weight, local_weight, local_bias):
    planes, modes_here = hidden_field.shape[0], spectral_weight.shape[0]
    devices = lax.axis_size("gx")
    lanes = planes * C
    zt_host = zt_tables(modes_here)
    zt, zt_turned = jnp.asarray(zt_host), jnp.asarray(np.ascontiguousarray(zt_host.T))
    y_table, y_back = jnp.asarray(y_forward_table()), jnp.asarray(y_inverse_table())
    mask = jnp.asarray(diagonal_mask())
    tables = [jnp.asarray(table) for table in x_tables(planes, devices)] + [mask]

    pick, same = jnp.asarray(row_pick()), jnp.asarray(same_y())
    bias = jnp.repeat(local_bias, YB)[:, None]

    def exchange(value):
        return lax.all_to_all(value, "gx", split_axis=0, concat_axis=0, tiled=True)

    def summed(value, span, end):
        while span < end:
            radix = 4 if 4 * span <= end else 2
            others = [
                lax.ppermute(value, "gx", [(d, d ^ (k * span)) for d in range(devices)])
                for k in range(1, radix)
            ]
            value = sum(others, value)
            span *= radix
        return value

    def to_owner(spectra):
        return exchange(spectra.reshape(devices, 2, modes_here, lanes))

    def to_slabs(back):
        return exchange(back).reshape(KY * 2 * Q, lanes)

    spectra = forward_planes(hidden_field, zt, y_table)
    zt, zt_turned, y_table, y_back = stage(zt, zt_turned, y_table, y_back)
    early = local_term(hidden_field, local_weight.T, bias, pick, same)
    back, modes = mix_modes(to_owner(spectra), spectral_weight, tables)
    output, slope, dspectra, bias_part = middle(
        to_slabs(back), early, cotangent, zt, zt_turned, y_back, y_table
    )
    total = pointwise_gradient(hidden_field, slope, bias_part, pick, same)
    dback, dmodes = adjoint_modes(to_owner(dspectra), spectral_weight, tables)
    near = min(devices, 8)
    total = summed(total, 1, near)
    dback, slope, total = lax.optimization_barrier((dback, slope, total))
    late = late_term(slope, local_weight, pick, same)
    grad_spectral = mode_gradient(modes, dmodes, mask)
    total = summed(total, near, devices)
    grad_field, grad_local, grad_bias = last(to_slabs(dback), late, zt_turned, y_back, total)
    grad_bias = grad_bias.reshape(C)
    return (output, grad_field, grad_spectral, grad_local, grad_bias)


def solution(mesh):
    placed = (
        P(("groups", "gx"), None, None, None),
        P(("groups", "gx"), None, None, None),
        P("gx", None, None, None),
        P(),
        P(),
    )
    return jax.shard_map(
        on_device,
        mesh=mesh,
        in_specs=placed,
        out_specs=(
            P(("groups", "gx"), None, None, None),
            P(("groups", "gx"), None, None, None),
            P("gx", "groups", None, None),
            P("groups", None),
            P("groups"),
        ),
        check_vma=False,
    )
```

```python
import functools
import math

import jax
import jax.numpy as jnp
import ml_dtypes
import numpy as np
from jax import lax
from jax.experimental import pallas as pl
from jax.experimental.pallas import tpu as pltpu
from jax.sharding import PartitionSpec as P

NX, NY, NZ, NT = 128, 64, 64, 8
KX, KY, KZ, KT = 16, 16, 16, 4
C = 32
Q = KZ * KT
CELLS = NZ * NT
YB = 16
PIECE = 16
AHEAD = 4
F32, BF16 = jnp.float32, jnp.bfloat16
HIGHEST = lax.Precision.HIGHEST
MIB = 1 << 20


def frequency(kept):
    serial = np.arange(kept)
    return np.where(serial < kept // 2, serial, serial - kept)


def angles(positions, length, kept):
    wound = (np.asarray(positions)[:, None] * frequency(kept)[None, :]) % length
    return 2.0 * math.pi / length * wound


def split2(table):
    high = table.astype(ml_dtypes.bfloat16)
    low = (table - high.astype(np.float64)).astype(ml_dtypes.bfloat16)
    return high, low


def stacked(table):
    high, low = split2(table)
    return np.concatenate([high, high, low], axis=1)


def zt_tables(modes_here):
    cells = np.arange(CELLS)
    depth, moment = cells // NT, cells % NT
    kept_z, kept_t = np.repeat(frequency(KZ), KT), np.tile(np.arange(KT), KZ)
    wound = (depth[:, None] * kept_z * NT + moment[:, None] * kept_t * NZ) % CELLS
    theta = 2.0 * math.pi / CELLS * wound
    cosine, sine = np.cos(theta), np.sin(theta)
    groups = Q // modes_here
    shape = (CELLS, groups, modes_here)
    cosine, sine = cosine.reshape(shape), sine.reshape(shape)
    first = np.stack([cosine, -sine], axis=2).reshape(CELLS, 2 * Q)
    second = np.stack([-sine, -cosine], axis=2).reshape(CELLS, 2 * Q)
    return np.concatenate([first, second], axis=1).astype(ml_dtypes.bfloat16)


def y_forward_table():
    theta = angles(np.arange(NY), NY, KY)
    table = np.concatenate([np.cos(theta), np.sin(theta)], axis=0).T
    high, low = split2(table)
    return np.concatenate([high, low], axis=0)


def y_inverse_table():
    theta = angles(np.arange(NY), NY, KY)
    table = np.concatenate([np.cos(theta), np.sin(theta)], axis=0)
    return stacked(table)


def x_tables(planes, devices):
    theta = angles(np.arange(devices) * planes, NX, KX).T
    cosine, sine = np.cos(theta), np.sin(theta)
    forward = np.block([[cosine, sine], [-sine, cosine]])
    turn = np.repeat(angles(np.arange(planes), NX, KX).T, C, axis=1)
    return (
        stacked(forward),
        stacked(forward.T),
        np.cos(turn).astype(np.float32),
        np.sin(turn).astype(np.float32),
    )


def diagonal_mask():
    return (np.arange(KX * C)[None, :] // C == np.arange(KX)[:, None]).astype(np.float32)


def halves(value):
    high = value.astype(BF16)
    return high, (value - high.astype(F32)).astype(BF16)


def three(value):
    high, low = halves(value)
    return jnp.concatenate([high, low, high], axis=0)


def dot(left, right):
    return jnp.dot(left, right, preferred_element_type=F32)


def lane_total(value, step):
    span = value.shape[1] // 2
    while span >= step:
        value = value + pltpu.roll(value, span, 1)
        span //= 2
    return value


def y_forward(sums, y_table, gathered, first_row, lanes):
    count = sums.shape[0] // NY
    for pair in range(0, count, 2):
        one = sums[pair * NY : (pair + 1) * NY].astype(BF16)
        two = sums[(pair + 1) * NY : (pair + 2) * NY].astype(BF16)
        right = jnp.concatenate(
            [
                jnp.concatenate([one[:, : 2 * Q], two[:, : 2 * Q]], axis=1),
                jnp.concatenate([one[:, 2 * Q :], two[:, 2 * Q :]], axis=1),
            ],
            axis=0,
        )
        both = dot(y_table, right)
        out = both[:KY] + both[KY:]
        gathered[pl.ds(first_row + pair, KY, stride=lanes), :] = out[:, : 2 * Q]
        gathered[pl.ds(first_row + pair + 1, KY, stride=lanes), :] = out[:, 2 * Q :]


def send_layout(gathered, out_ref, lanes):
    for ky in range(KY):
        out_ref[ky * 2 * Q : (ky + 1) * 2 * Q, :] = gathered[ky * lanes : (ky + 1) * lanes, :].T


def pieces(source, target, signals, plane, part):
    here = (plane, pl.ds(part * PIECE, PIECE))
    return pltpu.make_async_copy(
        source.at[here], target.at[here], signals.at[plane * (C // PIECE) + part]
    )


def plane_copies(source, target, signals, plane):
    return [pieces(source, target, signals, plane, part) for part in range(C // PIECE)]


def start_plane(source, target, signals, plane):
    for copy in plane_copies(source, target, signals, plane):
        copy.start()


def wait_plane(source, target, signals, plane):
    for copy in plane_copies(source, target, signals, plane):
        copy.wait()


def in_hbm():
    return pl.BlockSpec(memory_space=pl.ANY)


def in_vmem():
    return pl.BlockSpec(memory_space=pltpu.VMEM)


def forward_kernel(field, zt, y_table, out, buffer, gathered, arrived, *, lanes, group):
    planes = field.shape[0]
    for plane in range(min(AHEAD, planes)):
        start_plane(field, buffer, arrived, plane)

    def one_plane(plane, _):
        wait_plane(field, buffer, arrived, plane)

        @pl.when(plane + AHEAD < planes)
        def _():
            start_plane(field, buffer, arrived, plane + AHEAD)

        for c in range(0, C, group):
            values = buffer[plane, c : c + group].reshape(group * NY, CELLS)
            y_forward(dot(values, zt[...]), y_table[...], gathered, plane * C + c, lanes)
        return 0

    lax.fori_loop(0, planes, one_plane, 0)
    send_layout(gathered, out, lanes)


def forward_planes(field, zt, y_table, group=C):
    planes = field.shape[0]
    lanes = planes * C
    return pl.pallas_call(
        functools.partial(forward_kernel, lanes=lanes, group=group),
        in_specs=[in_hbm(), in_vmem(), in_vmem()],
        out_specs=in_vmem(),
        out_shape=jax.ShapeDtypeStruct((KY * 2 * Q, lanes), F32),
        scratch_shapes=[
            pltpu.VMEM(field.shape, BF16),
            pltpu.VMEM((KY * lanes, 2 * Q), F32),
            pltpu.SemaphoreType.DMA((planes * (C // PIECE),)),
        ],
        compiler_params=pltpu.CompilerParams(vmem_limit_bytes=56 * MIB),
        cost_estimate=pl.CostEstimate(flops=2 * 10**9, bytes_accessed=9 * MIB, transcendentals=0),
    )(field, zt, y_table)


Q_BLOCK = 16


def modes_of(received, q_count, devices, lanes, forward, cosine, sine):
    columns = []
    for q in range(q_count):
        parts = [
            received[pl.ds(ri * q_count + q, devices, stride=2 * q_count), :] for ri in range(2)
        ]
        columns.append(jnp.concatenate(parts, axis=0))
    right = jnp.concatenate(columns, axis=1) if lanes % 128 == 0 else None
    found = []
    if right is not None:
        summed = dot(forward, three(right))
    for q in range(q_count):
        if right is not None:
            one = summed[:, q * lanes : (q + 1) * lanes]
        else:
            one = dot(forward, three(columns[q]))
        a_re, a_im = one[:KX], one[KX:]
        m_re = lane_total(a_re * cosine + a_im * sine, C)
        m_im = lane_total(a_im * cosine - a_re * sine, C)
        found.append((m_re, m_im))
    return found


def to_planes(mixed, out, q_count, devices, lanes, inverse, cosine, sine):
    turned = []
    for re, im in mixed:
        turned.append(
            jnp.concatenate([re * cosine - im * sine, re * sine + im * cosine], axis=0)
        )
    if lanes % 128 == 0:
        joined = jnp.concatenate(turned, axis=1)
        back = dot(inverse, three(joined))
        backs = [back[:, q * lanes : (q + 1) * lanes] for q in range(q_count)]
    else:
        backs = [dot(inverse, three(one)) for one in turned]
    for q in range(q_count):
        for ri in range(2):
            out[pl.ds(ri * q_count + q, devices, stride=2 * q_count), :] = backs[q][
                ri * devices : (ri + 1) * devices
            ]


def mode_factor(first, q):
    time_frequency = lax.rem(first + q, KT)
    return jnp.where(time_frequency == 0, 1.0, 2.0).astype(F32) / (NX * NY * NZ * NT)


def beside(one, two):
    if one.shape[1] < 128:
        return jnp.concatenate([one, two], axis=1)
    lane = lax.broadcasted_iota(jnp.int32, one.shape, 1)
    return jnp.where(lane < C, one, two)[:, : 2 * C]


def mix_kernel(
    received, weight, forward, inverse, cosine, sine, mask, out, modes_out, *, devices, lanes
):
    q_block = weight.shape[0]
    first = pl.program_id(0) * q_block
    flat_in = received.reshape(devices * 2 * q_block, lanes)
    flat_out = out.reshape(devices * 2 * q_block, lanes)
    modes = modes_of(flat_in, q_block, devices, lanes, forward[...], cosine[...], sine[...])
    own_block = jnp.concatenate([mask[...]] * 2, axis=0)
    mixed = []
    for q in range(q_block):
        re, im = modes[q]
        modes_out[q] = jnp.concatenate([re, im], axis=0)
        high, low = halves(jnp.concatenate([beside(re, -im), beside(im, re)], axis=0))
        product = dot(jnp.concatenate([high, low], axis=0), weight[q].reshape(2 * C, KX * C))
        kept = (product[: 2 * KX] + product[2 * KX :]) * own_block
        total = kept[:, :128]
        for column in range(128, KX * C, 128):
            total = total + kept[:, column : column + 128]
        total = lane_total(total, C)[:, :lanes] * mode_factor(first, q)
        pieces = (total[:KX], total[KX:])
        mixed.append(pieces)
    to_planes(mixed, flat_out, q_block, devices, lanes, inverse[...], cosine[...], sine[...])


def stage_kernel(*refs):
    count = len(refs) // 2
    sources, places, done = refs[:count], refs[count : 2 * count], refs[-1]
    copies = [
        pltpu.make_async_copy(source, place, done.at[i])
        for i, (source, place) in enumerate(zip(sources, places))
    ]
    for copy in copies:
        copy.start()
    for copy in copies:
        copy.wait()


def stage(*arrays):
    return pl.pallas_call(
        stage_kernel,
        in_specs=[pl.BlockSpec(memory_space=pl.ANY)] * len(arrays),
        out_specs=[in_vmem() for _ in arrays],
        out_shape=[pltpu.VMEM(array.shape, array.dtype) for array in arrays],
        scratch_shapes=[pltpu.SemaphoreType.DMA((len(arrays),))],
        cost_estimate=pl.CostEstimate(flops=0, bytes_accessed=6 * MIB, transcendentals=0),
    )(*arrays)


def whole(array):
    return pl.BlockSpec(array.shape, lambda *_: (0,) * array.ndim)


def mode_specs(devices, modes_here, lanes):
    q_block = min(Q_BLOCK, modes_here)
    slab = pl.BlockSpec((devices, 2, q_block, lanes), lambda s: (0, 0, s, 0))
    weight = pl.BlockSpec((q_block, 2, C, KX * C), lambda s: (s, 0, 0, 0))
    modes = pl.BlockSpec((q_block, 2 * KX, lanes), lambda s: (s, 0, 0))
    return slab, weight, modes


def mix_modes(received, weight, tables):
    devices, _, modes_here, lanes = received.shape
    slab, weight_spec, modes = mode_specs(devices, modes_here, lanes)
    return pl.pallas_call(
        functools.partial(mix_kernel, devices=devices, lanes=lanes),
        grid=(modes_here // min(Q_BLOCK, modes_here),),
        in_specs=[slab, weight_spec] + [whole(table) for table in tables],
        out_specs=[slab, modes],
        out_shape=[
            jax.ShapeDtypeStruct(received.shape, F32),
            jax.ShapeDtypeStruct((modes_here, 2 * KX, lanes), F32),
        ],
        compiler_params=pltpu.CompilerParams(vmem_limit_bytes=32 * MIB),
        cost_estimate=pl.CostEstimate(flops=10**9, bytes_accessed=5 * MIB, transcendentals=0),
    )(received, weight, *tables)


def spread(value, mask):
    if value.shape[1] < 128:
        value = jnp.concatenate([value] * (128 // value.shape[1]), axis=1)
    else:
        value = value[:, :128]
    return jnp.concatenate([value] * (KX * C // 128), axis=1) * mask


def adjoint_kernel(
    received, weight, forward, inverse, cosine, sine, mask, out, modes_out, *, devices, lanes
):
    q_block = weight.shape[0]
    first = pl.program_id(0) * q_block
    flat_in = received.reshape(devices * 2 * q_block, lanes)
    flat_out = out.reshape(devices * 2 * q_block, lanes)
    modes = modes_of(flat_in, q_block, devices, lanes, forward[...], cosine[...], sine[...])
    group = lax.broadcasted_iota(jnp.int32, (KX, 128), 1) // C
    odd = group % 2 == 1
    mixed = []
    for q in range(q_block):
        factor = mode_factor(first, q)
        d_re, d_im = modes[q][0] * factor, modes[q][1] * factor
        modes_out[q] = jnp.concatenate([d_re, d_im], axis=0)
        wide = jnp.concatenate([spread(d_re, mask[...]), spread(d_im, mask[...])], axis=0)
        high, low = halves(wide)
        left = jnp.concatenate([high, low], axis=0)
        right = jnp.concatenate([weight[q, 0], weight[q, 1]] * 2, axis=0)
        product = lax.dot_general(
            left, right, (((1,), (1,)), ((), ())), preferred_element_type=F32
        )
        product = product[: 2 * KX] + product[2 * KX :]
        re = product[:KX] + pltpu.roll(product[KX:], 128 - C, 1)
        im = product[KX:] - pltpu.roll(product[:KX], 128 - C, 1)
        re = jnp.where(odd, pltpu.roll(re, C, 1), re)
        im = jnp.where(odd, pltpu.roll(im, C, 1), im)
        mixed.append((re[:, :lanes], im[:, :lanes]))
    to_planes(mixed, flat_out, q_block, devices, lanes, inverse[...], cosine[...], sine[...])


def adjoint_modes(received, weight, tables):
    devices, _, modes_here, lanes = received.shape
    slab, weight_spec, modes = mode_specs(devices, modes_here, lanes)
    return pl.pallas_call(
        functools.partial(adjoint_kernel, devices=devices, lanes=lanes),
        grid=(modes_here // min(Q_BLOCK, modes_here),),
        in_specs=[slab, weight_spec] + [whole(table) for table in tables],
        out_specs=[slab, modes],
        out_shape=[
            jax.ShapeDtypeStruct(received.shape, F32),
            jax.ShapeDtypeStruct((modes_here, 2 * KX, lanes), F32),
        ],
        compiler_params=pltpu.CompilerParams(vmem_limit_bytes=32 * MIB),
        cost_estimate=pl.CostEstimate(flops=10**9, bytes_accessed=5 * MIB, transcendentals=0),
    )(received, weight, *tables)


def gradient_kernel(modes, dmodes, mask, out):
    for q in range(modes.shape[0]):
        left = modes[q][:, :C]
        l_high, l_low = halves(left)
        left = jnp.concatenate([l_high, l_high, l_low], axis=0)
        d_re, d_im = spread(dmodes[q, :KX], mask[...]), spread(dmodes[q, KX:], mask[...])
        for part, rows in ((0, (d_re, d_im)), (1, (d_im, -d_re))):
            high, low = halves(jnp.concatenate(rows, axis=0))
            right = jnp.concatenate([high, low, high], axis=0)
            out[q, part] = lax.dot_general(
                left, right, (((0,), (0,)), ((), ())), preferred_element_type=F32
            )


def mode_gradient(modes, dmodes, mask):
    modes_here, _, lanes = modes.shape
    q_block = min(Q_BLOCK, modes_here)
    spec = pl.BlockSpec((q_block, 2 * KX, lanes), lambda s: (s, 0, 0))
    return pl.pallas_call(
        gradient_kernel,
        grid=(modes_here // q_block,),
        in_specs=[spec, spec, whole(mask)],
        out_specs=pl.BlockSpec((q_block, 2, C, KX * C), lambda s: (s, 0, 0, 0)),
        out_shape=jax.ShapeDtypeStruct((modes_here, 2, C, KX * C), F32),
        compiler_params=pltpu.CompilerParams(vmem_limit_bytes=32 * MIB),
        cost_estimate=pl.CostEstimate(flops=10**8, bytes_accessed=5 * MIB, transcendentals=0),
    )(modes, dmodes, mask)


def planes_layout(back, gathered, lanes):
    for ky in range(KY):
        gathered[ky * lanes : (ky + 1) * lanes, :] = back[ky * 2 * Q : (ky + 1) * 2 * Q, :].T


def y_inverse(gathered, y_table, first_row, count, lanes):
    found = []
    for c in range(0, count, 2):
        row = first_row + c
        pair = jnp.concatenate(
            [
                gathered[pl.ds(row, KY, stride=lanes), :],
                gathered[pl.ds(row + 1, KY, stride=lanes), :],
            ],
            axis=1,
        )
        both = dot(y_table, three(pair)).astype(BF16)
        for k in range(2):
            columns = slice(k * 2 * Q, (k + 1) * 2 * Q)
            found.append(jnp.concatenate([both[:NY, columns], both[NY:, columns]], axis=1))
    return jnp.concatenate(found, axis=0)


def row_pick():
    return (np.arange(C * YB)[:, None] // YB == np.arange(C)[None, :]).astype(ml_dtypes.bfloat16)


def same_y():
    rows = np.arange(C * YB)
    return (rows[:, None] % YB == rows[None, :] % YB).astype(ml_dtypes.bfloat16)


def channel_map(weight, pick, same, out):
    rows = dot(pick, weight).astype(BF16)
    wide = lax.dot_general(rows, pick, (((1,), (1,)), ((), ())), preferred_element_type=F32)
    out[...] = wide.astype(BF16) * same


def local_kernel(field, weight, bias, pick, same, out, local):
    rows = C * YB

    @pl.when((pl.program_id(0) == 0) & (pl.program_id(1) == 0))
    def _():
        channel_map(weight[...], pick[...], same[...], local)

    for part in range(field.shape[2] // YB):
        y = slice(part * YB, (part + 1) * YB)
        total = dot(local[...], field[0, :, y].reshape(rows, CELLS)) + bias[...]
        out[0, :, y] = total.astype(BF16).reshape(C, YB, CELLS)


def local_term(field, weight, bias, pick, same, parts=1):
    block = pl.BlockSpec((1, C, NY // parts, CELLS), lambda x, y: (x, 0, y, 0))
    rows = C * YB
    return pl.pallas_call(
        local_kernel,
        grid=(field.shape[0], parts),
        in_specs=[block, whole(weight), whole(bias), whole(pick), whole(same)],
        out_specs=block,
        out_shape=jax.ShapeDtypeStruct(field.shape, BF16),
        scratch_shapes=[pltpu.VMEM((rows, rows), BF16)],
        compiler_params=pltpu.CompilerParams(vmem_limit_bytes=56 * MIB),
        cost_estimate=pl.CostEstimate(flops=4 * 10**9, bytes_accessed=17 * MIB, transcendentals=0),
    )(field, weight, bias, pick, same)


def late_kernel(slope, weight, pick, same, out, local):
    rows = C * YB

    @pl.when((pl.program_id(0) == 0) & (pl.program_id(1) == 0))
    def _():
        channel_map(weight[...], pick[...], same[...], local)

    for part in range(slope.shape[2] // YB):
        y = slice(part * YB, (part + 1) * YB)
        total = dot(local[...], slope[0, :, y].reshape(rows, CELLS))
        out[0, :, y] = total.astype(BF16).reshape(C, YB, CELLS)


def late_term(slope, weight, pick, same, parts=1):
    block = pl.BlockSpec((1, C, NY // parts, CELLS), lambda x, y: (x, 0, y, 0))
    rows = C * YB
    return pl.pallas_call(
        late_kernel,
        grid=(slope.shape[0], parts),
        in_specs=[block, whole(weight), whole(pick), whole(same)],
        out_specs=block,
        out_shape=jax.ShapeDtypeStruct(slope.shape, BF16),
        scratch_shapes=[pltpu.VMEM((rows, rows), BF16)],
        compiler_params=pltpu.CompilerParams(vmem_limit_bytes=56 * MIB),
        cost_estimate=pl.CostEstimate(flops=4 * 10**9, bytes_accessed=17 * MIB, transcendentals=0),
    )(slope, weight, pick, same)


def pointwise_kernel(field, slope, bias_part, pick, same, out, total):
    rows = C * YB
    first_step = (pl.program_id(0) == 0) & (pl.program_id(1) == 0)
    last_step = (pl.program_id(0) == pl.num_programs(0) - 1) & (
        pl.program_id(1) == pl.num_programs(1) - 1
    )

    @pl.when(first_step)
    def _():
        total[...] = jnp.zeros_like(total)

    for part in range(field.shape[2] // YB):
        y = slice(part * YB, (part + 1) * YB)
        total[...] += lax.dot_general(
            field[0, :, y].reshape(rows, CELLS),
            slope[0, :, y].reshape(rows, CELLS),
            (((1,), (1,)), ((), ())),
            preferred_element_type=F32,
        )

    @pl.when(last_step)
    def _():
        to_f32 = functools.partial(
            lax.dot_general, precision=HIGHEST, preferred_element_type=F32
        )
        chosen = pick[...].astype(F32)
        tiled = jnp.concatenate([chosen] * 4, axis=1)
        kept = total[...] * same[...].astype(F32)
        across = to_f32(kept, tiled, (((1,), (0,)), ((), ())))
        grads = to_f32(chosen, across, (((0,), (0,)), ((), ())))
        out[:C, :] = grads
        lane_sums = to_f32(jnp.ones((8, 128), F32), bias_part[...], (((1,), (1,)), ((), ())))
        by_channel = (
            lax.broadcasted_iota(jnp.int32, (8 * C, 128), 0) // 8
            == lax.broadcasted_iota(jnp.int32, (8 * C, 128), 1)
        ).astype(F32)
        out[C:, :] = to_f32(lane_sums, by_channel, (((1,), (0,)), ((), ())))


def pointwise_gradient(field, slope, bias_part, pick, same, parts=1):
    block = pl.BlockSpec((1, C, NY // parts, CELLS), lambda x, y: (x, 0, y, 0))
    rows = C * YB
    return pl.pallas_call(
        pointwise_kernel,
        grid=(field.shape[0], parts),
        in_specs=[block, block, whole(bias_part), whole(pick), whole(same)],
        out_specs=pl.BlockSpec((C + 8, 128), lambda x, y: (0, 0)),
        out_shape=jax.ShapeDtypeStruct((C + 8, 128), F32),
        scratch_shapes=[pltpu.VMEM((rows, rows), F32)],
        compiler_params=pltpu.CompilerParams(vmem_limit_bytes=56 * MIB),
        cost_estimate=pl.CostEstimate(flops=4 * 10**9, bytes_accessed=17 * MIB, transcendentals=0),
    )(field, slope, bias_part, pick, same)


def middle_kernel(
    back,
    early,
    cotangent,
    zt,
    zt_turned,
    y_back,
    y_table,
    out,
    slope_out,
    spectra,
    bias_grad,
    left,
    right,
    gathered,
    collected,
    left_in,
    right_in,
    left_out,
    right_out,
    *,
    lanes,
    group,
):
    planes = cotangent.shape[0]
    for plane in range(min(AHEAD, planes)):
        start_plane(early, left, left_in, plane)
        start_plane(cotangent, right, right_in, plane)
    planes_layout(back, gathered, lanes)
    bias_grad[...] = jnp.zeros_like(bias_grad)
    half_root = 1.0 / math.sqrt(2.0)

    def one_plane(plane, _):
        wait_plane(early, left, left_in, plane)
        wait_plane(cotangent, right, right_in, plane)

        @pl.when(plane + AHEAD < planes)
        def _():
            start_plane(early, left, left_in, plane + AHEAD)
            start_plane(cotangent, right, right_in, plane + AHEAD)

        for g in range(0, C, group):
            own = y_inverse(gathered, y_back[...], plane * C + g, group, lanes)
            pre = dot(own, zt_turned[...])
            parts = range(g // PIECE, (g + group) // PIECE)
            low = []
            for c in range(group):
                v = pre[c * NY : (c + 1) * NY] + left[plane, g + c].astype(F32)
                grade = right[plane, g + c].astype(F32)
                normal = 0.5 + 0.5 * lax.erf(v * half_root)
                left[plane, g + c] = (v * normal).astype(BF16)
                bell = jnp.exp(-0.5 * v * v) * (1.0 / math.sqrt(2.0 * math.pi))
                slope = grade * (normal + v * bell)
                low.append(slope.astype(BF16))
                right[plane, g + c] = low[-1]
                folded = slope[:, :128]
                for column in range(128, CELLS, 128):
                    folded = folded + slope[:, column : column + 128]
                total = folded[:8]
                for row in range(8, NY, 8):
                    total = total + folded[row : row + 8]
                bias_grad[(g + c) * 8 : (g + c + 1) * 8, :] += total
            for part in parts:
                pieces(left, out, left_out, plane, part).start()
                pieces(right, slope_out, right_out, plane, part).start()
            sums = dot(jnp.concatenate(low, axis=0), zt[...])
            y_forward(sums, y_table[...], collected, plane * C + g, lanes)
        return 0

    lax.fori_loop(0, planes, one_plane, 0)
    send_layout(collected, spectra, lanes)
    for plane in range(planes):
        wait_plane(left, out, left_out, plane)
        wait_plane(right, slope_out, right_out, plane)


def middle(back, early, cotangent, zt, zt_turned, y_back, y_table, group=C):
    planes = cotangent.shape[0]
    lanes = planes * C
    signals = pltpu.SemaphoreType.DMA((planes * (C // PIECE),))
    return pl.pallas_call(
        functools.partial(middle_kernel, lanes=lanes, group=group),
        in_specs=[in_vmem(), in_hbm(), in_hbm()] + [in_vmem()] * 4,
        out_specs=[in_hbm(), in_hbm(), in_vmem(), in_vmem()],
        out_shape=[
            jax.ShapeDtypeStruct(cotangent.shape, BF16),
            jax.ShapeDtypeStruct(cotangent.shape, BF16),
            jax.ShapeDtypeStruct((KY * 2 * Q, lanes), F32),
            jax.ShapeDtypeStruct((C * 8, 128), F32),
        ],
        scratch_shapes=[
            pltpu.VMEM(cotangent.shape, BF16),
            pltpu.VMEM(cotangent.shape, BF16),
            pltpu.VMEM((KY * lanes, 2 * Q), F32),
            pltpu.VMEM((KY * lanes, 2 * Q), F32),
            signals,
            signals,
            signals,
            signals,
        ],
        compiler_params=pltpu.CompilerParams(vmem_limit_bytes=48 * MIB),
        cost_estimate=pl.CostEstimate(
            flops=5 * 10**9, bytes_accessed=34 * MIB, transcendentals=8 * 10**6
        ),
    )(back, early, cotangent, zt, zt_turned, y_back, y_table)


def last_kernel(
    back,
    early,
    zt_turned,
    y_back,
    sums,
    out,
    local_grad,
    bias_grad,
    buffer,
    gathered,
    arrived,
    left,
    *,
    lanes,
    group,
):
    planes = early.shape[0]
    for plane in range(min(AHEAD, planes)):
        start_plane(early, buffer, arrived, plane)
    planes_layout(back, gathered, lanes)
    local_grad[...] = sums[:C, :C]
    bias_grad[...] = sums[C : C + 1, :C]

    def one_plane(plane, _):
        wait_plane(early, buffer, arrived, plane)

        @pl.when(plane + AHEAD < planes)
        def _():
            start_plane(early, buffer, arrived, plane + AHEAD)

        for g in range(0, C, group):
            own = y_inverse(gathered, y_back[...], plane * C + g, group, lanes)
            total = dot(own, zt_turned[...]).reshape(group, NY, CELLS)
            here = slice(g, g + group)
            buffer[plane, here] = (total + buffer[plane, here].astype(F32)).astype(BF16)
            for part in range(g // PIECE, (g + group) // PIECE):
                pieces(buffer, out, left, plane, part).start()
        return 0

    lax.fori_loop(0, planes, one_plane, 0)
    for plane in range(planes):
        wait_plane(buffer, out, left, plane)


def last(back, early, zt_turned, y_back, sums, group=C):
    planes = early.shape[0]
    lanes = planes * C
    signals = pltpu.SemaphoreType.DMA((planes * (C // PIECE),))
    return pl.pallas_call(
        functools.partial(last_kernel, lanes=lanes, group=group),
        in_specs=[in_vmem(), in_hbm(), in_vmem(), in_vmem(), in_vmem()],
        out_specs=[in_hbm(), in_vmem(), in_vmem()],
        out_shape=[
            jax.ShapeDtypeStruct(early.shape, BF16),
            jax.ShapeDtypeStruct((C, C), F32),
            jax.ShapeDtypeStruct((1, C), F32),
        ],
        scratch_shapes=[
            pltpu.VMEM(early.shape, BF16),
            pltpu.VMEM((KY * lanes, 2 * Q), F32),
            signals,
            signals,
        ],
        compiler_params=pltpu.CompilerParams(vmem_limit_bytes=52 * MIB),
        cost_estimate=pl.CostEstimate(
            flops=2 * 10**9, bytes_accessed=17 * MIB, transcendentals=0
        ),
    )(back, early, zt_turned, y_back, sums)


def on_device(hidden_field, cotangent, spectral_weight, local_weight, local_bias):
    planes, modes_here = hidden_field.shape[0], spectral_weight.shape[0]
    devices = lax.axis_size("gx")
    lanes = planes * C
    zt_host = zt_tables(modes_here)
    zt, zt_turned = jnp.asarray(zt_host), jnp.asarray(np.ascontiguousarray(zt_host.T))
    y_table, y_back = jnp.asarray(y_forward_table()), jnp.asarray(y_inverse_table())
    mask = jnp.asarray(diagonal_mask())
    tables = [jnp.asarray(table) for table in x_tables(planes, devices)] + [mask]

    pick, same = jnp.asarray(row_pick()), jnp.asarray(same_y())
    bias = jnp.repeat(local_bias, YB)[:, None]

    def exchange(value):
        return lax.all_to_all(value, "gx", split_axis=0, concat_axis=0, tiled=True)

    def summed(value, span, end):
        while span < end:
            radix = 4 if 4 * span <= end else 2
            others = [
                lax.ppermute(value, "gx", [(d, d ^ (k * span)) for d in range(devices)])
                for k in range(1, radix)
            ]
            value = sum(others, value)
            span *= radix
        return value

    def to_owner(spectra):
        return exchange(spectra.reshape(devices, 2, modes_here, lanes))

    def to_slabs(back):
        return exchange(back).reshape(KY * 2 * Q, lanes)

    spectra = forward_planes(hidden_field, zt, y_table)
    zt, zt_turned, y_table, y_back = stage(zt, zt_turned, y_table, y_back)
    early = local_term(hidden_field, local_weight.T, bias, pick, same)
    back, modes = mix_modes(to_owner(spectra), spectral_weight, tables)
    output, slope, dspectra, bias_part = middle(
        to_slabs(back), early, cotangent, zt, zt_turned, y_back, y_table
    )
    total = pointwise_gradient(hidden_field, slope, bias_part, pick, same)
    dback, dmodes = adjoint_modes(to_owner(dspectra), spectral_weight, tables)
    near = min(devices, 16)
    total = summed(total, 1, near)
    dback, slope, total = lax.optimization_barrier((dback, slope, total))
    late = late_term(slope, local_weight, pick, same)
    grad_spectral = mode_gradient(modes, dmodes, mask)
    total = summed(total, near, devices)
    grad_field, grad_local, grad_bias = last(to_slabs(dback), late, zt_turned, y_back, total)
    grad_bias = grad_bias.reshape(C)
    return (output, grad_field, grad_spectral, grad_local, grad_bias)


def solution(mesh):
    placed = (
        P(("groups", "gx"), None, None, None),
        P(("groups", "gx"), None, None, None),
        P("gx", None, None, None),
        P(),
        P(),
    )
    return jax.shard_map(
        on_device,
        mesh=mesh,
        in_specs=placed,
        out_specs=(
            P(("groups", "gx"), None, None, None),
            P(("groups", "gx"), None, None, None),
            P("gx", "groups", None, None),
            P("groups", None),
            P("groups"),
        ),
        check_vma=False,
    )
```
